32 devices in a mesh: gz: 4 (over y, core), gx: 2 (over x), gy: 4 (over z).
Axes of the slice: x: 2, y: 2, z: 4, core: 2. Of those that a mesh axis runs over, the one named last changes fastest.
Arguments:
- initial_field: float32 [8, 256, 512], P('gz', 'gx', 'gy'), may hold values from -6 to 6
- source_term: float32 [8, 256, 512], P('gz', 'gx', 'gy'), may hold values from -48 to 48
- block_inverse: float32 [256, 512, 128], P('gx', 'gy'), may hold values from -0.1 to 0.1
Outputs:
- smoothed: float32 [8, 256, 512], P('gz', 'gx', 'gy')
The draws below stay inside these ranges and needn't reach their ends.
All inputs are finite; a program needn't handle non-finite values.
Results may differ from the reference program's by a relative error of at most 0.00013.
Values sent between devices are 32-bit elements; how exact they have to be, the bound alone decides.
No kernel may reach another device: no remote copies, remote signals or barrier semaphores. Data moves between devices by JAX's collectives and lax.ppermute only.
A program may use at most 64 MiB of HBM per device.

```python
import math
import jax
import jax.numpy as jnp
from jax import lax

LINE = 128
NZ = 8
NX = 256
NY = 512


def smooth_wave(key, grid_shape, first_axis, first_count, second_axis, second_count):
    phases = jax.random.uniform(key, (2,), jnp.float32, -math.pi, math.pi)
    first_pos = lax.broadcasted_iota(jnp.float32, grid_shape, first_axis) * (2.0 * math.pi / first_count)
    second_pos = lax.broadcasted_iota(jnp.float32, grid_shape, second_axis) * (2.0 * math.pi / second_count)
    return jnp.cos(first_pos + phases[0]) * jnp.cos(second_pos + phases[1])


def draw_initial_field(key, part):
    wave_key, noise_key = jax.random.split(jax.random.fold_in(key, 21))
    grid_shape = (NZ, NX, NY)
    wave_part = smooth_wave(wave_key, grid_shape, 1, NX, 0, NZ)
    smooth_part = -2.0 * (1.0 + 0.4 * wave_part)
    noise_part = jnp.clip(jax.random.normal(noise_key, grid_shape, jnp.float32), -3.0, 3.0)
    return (smooth_part + noise_part).astype(jnp.float32)


def draw_source_term(key, part):
    wave_key, noise_key = jax.random.split(jax.random.fold_in(key, 31))
    grid_shape = (NZ, NX, NY)
    wave_part = smooth_wave(wave_key, grid_shape, 1, NX, 2, NY)
    smooth_part = 10.0 * (1.0 + 0.5 * wave_part)
    noise_part = jnp.clip(8.0 * jax.random.normal(noise_key, grid_shape, jnp.float32), -30.0, 30.0)
    return (smooth_part + noise_part).astype(jnp.float32)


def draw_block_inverse(key, part):
    first_key, second_key = jax.random.split(jax.random.fold_in(key, 11))
    row_index = lax.broadcasted_iota(jnp.int32, (NX, NY, LINE), 1) % LINE
    col_index = lax.broadcasted_iota(jnp.int32, (NX, NY, LINE), 2)
    strength = jnp.exp(jax.random.uniform(first_key, (NX, NY, 1), jnp.float32, math.log(1.2), math.log(1.9)))
    spread = jnp.clip(jax.random.normal(second_key, (NX, NY, LINE), jnp.float32), -5.0, 5.0)
    diagonal_part = jnp.where(row_index == col_index, strength, 0.0)
    off_part = spread * (0.4 / math.sqrt(LINE))
    return ((diagonal_part + off_part) / 26.0).astype(jnp.float32)


def setup_inputs(seed: int = 0) -> dict:
    arg_keys = jax.random.split(jax.random.key(seed), 4)
    return {
        "initial_field": draw_initial_field(jax.random.fold_in(arg_keys[3], 71), 0),
        "source_term": draw_source_term(jax.random.fold_in(arg_keys[3], 71), 0),
        "block_inverse": draw_block_inverse(jax.random.fold_in(arg_keys[3], 71), 0),
    }


exact_mode = lax.Precision.HIGHEST


def box_sum(plane):
    padded = jnp.pad(plane, 1)
    row_sums = padded[:-2] + padded[1:-1] + padded[2:]
    return row_sums[:, :-2] + row_sums[:, 1:-1] + row_sums[:, 2:]


def apply_blocks(block_inverse, residual):
    count_x, count_y = residual.shape
    width = block_inverse.shape[2]
    lines = residual.reshape(count_x, count_y // width, width)
    blocks = block_inverse.reshape(count_x, count_y // width, width, width)
    return jnp.einsum("xqij,xqj->xqi", blocks, lines, precision=exact_mode).reshape(count_x, count_y)


def sweep_planes(field_now, source_term, block_inverse, backward):
    padded = jnp.pad(field_now, ((1, 1), (0, 0), (0, 0)))

    def update_plane(step, padded):
        if backward:
            zindex = (NZ - 1 - step).astype(jnp.int32)
        else:
            zindex = jnp.asarray(step).astype(jnp.int32)
        triple = lax.dynamic_slice_in_dim(padded, zindex, 3, 0)
        neighbours = box_sum(triple[0]) + box_sum(triple[1]) + box_sum(triple[2])
        source_plane = lax.dynamic_index_in_dim(source_term, zindex, 0, keepdims=False)
        residual = source_plane - (27.0 * triple[1] - neighbours)
        fresh = triple[1] + apply_blocks(block_inverse, residual)
        return lax.dynamic_update_slice_in_dim(padded, fresh[None], zindex + 1, 0)

    padded = lax.fori_loop(0, NZ, update_plane, padded)
    return padded[1:-1]


def reference(initial_field, source_term, block_inverse):
    forward = sweep_planes(initial_field, source_term, block_inverse, False)
    return sweep_planes(forward, source_term, block_inverse, True)
```

```python
import functools
import math
import jax
import jax.numpy as jnp
from jax import lax
from jax.experimental import pallas as pl
from jax.experimental.pallas import tpu as pltpu
from jax.sharding import PartitionSpec as P

LANES = 128
HALF = 64
STEPS = 4
SPREAD = [(k, side, delta) for k in range(1, STEPS) for side in range(2) for delta in range(1 - k, k)]
PACK_ROWS = 8 * (-(-(STEPS + len(SPREAD)) // 8))
VMEM = pl.BlockSpec(memory_space=pltpu.VMEM)
ANY = pl.BlockSpec(memory_space=pl.ANY)
PARAMS = pltpu.CompilerParams(vmem_limit_bytes=40 * 1024 * 1024)


def low_lanes(rows):
    return lax.broadcasted_iota(jnp.int32, (rows, LANES), 1) < HALF


def swap_halves(a):
    return pltpu.roll(a, HALF, 1)


def from_line(a, delta):
    return a if delta == 0 else pltpu.roll(a, (-delta) % LANES, 1)


def sum_x(a):
    return a + pltpu.roll(a, 1, 1) + pltpu.roll(a, LANES - 1, 1)


def sum_y(a, halo=None):
    low = low_lanes(1)
    first = swap_halves(a[:8])[0:1]
    last = swap_halves(a[HALF - 8 :])[7:8]
    halo = jnp.zeros((1, LANES), jnp.float32) if halo is None else halo
    above = jnp.where(low, halo, last)
    below = jnp.where(low, first, halo)
    row = lax.broadcasted_iota(jnp.int32, a.shape, 0)
    up = jnp.where(row == 0, above, pltpu.roll(a, 1, 0))
    down = jnp.where(row == HALF - 1, below, pltpu.roll(a, HALF - 1, 0))
    return a + up + down


def spread(a):
    low = low_lanes(a.shape[0])
    swapped = swap_halves(a)
    return jnp.where(low, a, swapped), jnp.where(low, swapped, a)


def edges(a):
    return jnp.where(low_lanes(1), a[0:1], a[HALF - 1 : HALF])


def block(b_ref, j):
    return b_ref[pl.ds(pl.multiple_of(j * HALF, HALF), HALF), :]


def apply_blocks(b_ref, rhs, r_refs):
    count = len(rhs)
    for a, r_ref in zip(rhs, r_refs):
        r_ref[0:HALF, :], r_ref[HALF:LANES, :] = spread(a)
    unroll = 8 if count == 1 else 2

    def step(outer, totals):
        totals = list(totals)
        for u in range(unroll):
            j = outer * unroll + u
            rows = block(b_ref, j)
            for n in range(count):
                slot = n if count > 1 else u % 2
                totals[slot] = totals[slot] + rows * r_refs[n][pl.ds(j, 1), :]
        return tuple(totals)

    zero = jnp.zeros((HALF, LANES), jnp.float32)
    totals = lax.fori_loop(0, LANES // unroll, step, (zero,) * max(2, count))
    return [totals[0] + totals[1]] if count == 1 else list(totals)


def layout_kernel(own, axis, b_ref, ghost_ref, out_ref, window, sems):
    ghost = ghost_ref.shape[0] // LANES
    count = b_ref.shape[0] // LANES
    position = lax.axis_index(axis)
    chunk = math.gcd(own, ghost)
    size = chunk * LANES
    copies = []
    for c in range(HALF // chunk):
        start = position * own - ghost + c * chunk
        inside = jnp.logical_and(start >= 0, start < count)
        target = window.at[pl.ds(c * size, size)]
        here = jnp.clip(start, 0, count - chunk)
        beyond = jnp.clip(jnp.where(start < 0, start + ghost, start - count), 0, ghost - chunk)

        @pl.when(inside)
        def _(at=pl.multiple_of(here * LANES, LANES), target=target, c=c):
            pltpu.make_async_copy(b_ref.at[pl.ds(at, size)], target, sems.at[c]).start()

        @pl.when(jnp.logical_not(inside))
        def _(at=pl.multiple_of(beyond * LANES, LANES), target=target, c=c):
            pltpu.make_async_copy(ghost_ref.at[pl.ds(at, size)], target, sems.at[c]).start()

        copies.append(pltpu.make_async_copy(b_ref.at[pl.ds(0, size)], target, sems.at[c]))
    for copy in copies:
        copy.wait()

    def one(i, carry):
        top = window[pl.ds(i, HALF, stride=LANES), :]
        bottom = window[pl.ds(i + HALF, HALF, stride=LANES), :]
        out_ref[pl.ds(i, LANES, stride=HALF), :] = jnp.concatenate([top, bottom], axis=0).T
        return carry

    lax.fori_loop(0, HALF, one, 0)


def responses(b_ref, r_refs, pack_ref):
    low_all = low_lanes(LANES)
    edge_rows = jnp.where(
        low_all,
        b_ref[pl.ds(0, LANES, stride=HALF), :],
        b_ref[pl.ds(HALF - 1, LANES, stride=HALF), :],
    )
    firsts = [block(b_ref, 0), block(b_ref, LANES - 1)]
    shifted = [sum_y(a) for a in firsts]
    plan = [(side, delta) for side in range(2) for delta in (-1, 0, 1)]
    seconds = apply_blocks(b_ref, [from_line(shifted[side], delta) for side, delta in plan], r_refs)
    second = {key: value for key, value in zip(plan, seconds)}
    for n, (k, side, delta) in enumerate(SPREAD):
        if k == 1:
            row = edges(firsts[side])
        elif k == 2:
            row = edges(second[side, delta])
        else:
            parts = [
                from_line(second[side, delta - m], m) for m in (-1, 0, 1) if abs(delta - m) <= 1
            ]
            top, bottom = spread(sum_y(sum(parts[1:], parts[0])))
            row = jnp.sum(edge_rows[:HALF] * top + edge_rows[HALF:] * bottom, axis=0, keepdims=True)
        pack_ref[pl.ds(STEPS + n, 1), :] = row


def local_chain(steps, b_ref, rhs_ref, add_ref, state, r_refs, pack_ref, first_loc_ref):
    nz = rhs_ref.shape[0]
    if state is not None:
        pack_ref[0:1, :] = edges(state)
    for n, step in enumerate(steps[:-1]):
        z = step if step < nz else 2 * nz - 1 - step
        rhs = rhs_ref[z]
        if state is not None:
            rhs = rhs + sum_y(sum_x(state))
        (state,) = apply_blocks(b_ref, [rhs], r_refs)
        if step >= nz:
            state = state + add_ref[z]
        if n == 0:
            first_loc_ref[...] = state
        pack_ref[n + 1 : n + 2, :] = edges(state)


def gather_planes(axis, field_refs, v_ref, s_ref):
    position = lax.axis_index(axis)
    low = low_lanes(HALF)
    nz_local = field_refs[0].shape[1]
    for k, ref in enumerate(field_refs):
        base = jnp.bitwise_xor(position, k) * nz_local
        for p in range(nz_local):
            for kind, target in ((0, v_ref), (1, s_ref)):
                plane = ref[kind, p]
                turned = jnp.concatenate([plane, plane], axis=0).T
                target[base + p + 1 - kind] = jnp.where(low, turned[:HALF], turned[HALF:])


def first_kernel(axis, fields, *refs):
    field_refs = refs[:fields]
    b_ref, rhs_ref, loc_ref, pack_ref, v_ref, s_ref = refs[fields : fields + 6]
    r_refs = refs[fields + 6 :]
    nz = rhs_ref.shape[0]
    pack_ref[...] = jnp.zeros(pack_ref.shape, jnp.float32)
    responses(b_ref, r_refs, pack_ref)
    v_ref[0] = jnp.zeros((HALF, LANES), jnp.float32)
    v_ref[nz + 1] = jnp.zeros((HALF, LANES), jnp.float32)
    gather_planes(axis, field_refs, v_ref, s_ref)
    for z in range(nz):
        around = v_ref[z] + v_ref[z + 1] + v_ref[z + 2]
        rhs_ref[z] = s_ref[z] - 27.0 * v_ref[z + 1] + sum_y(sum_x(around))
        pack_ref[PACK_ROWS + z : PACK_ROWS + z + 1, :] = edges(around)
    local_chain(list(range(STEPS)), b_ref, rhs_ref, None, None, r_refs, pack_ref, loc_ref)


def halo_of(ends):
    swapped = swap_halves(ends)
    return sum_x(jnp.where(low_lanes(8), pltpu.roll(swapped, 1, 0), pltpu.roll(swapped, 7, 0)))


def lines_both(row):
    swapped = swap_halves(row)
    low = low_lanes(8)
    return jnp.where(low, row, swapped), jnp.where(low, swapped, row)


def complete_edges(first, gather, coef_ref, halo_ref, inject_ref):
    injected = []
    ends = None if first else gather[:, 0, :]
    for t in range(STEPS):
        halo = jnp.zeros((8, LANES), jnp.float32) if ends is None else halo_of(ends)
        halo_ref[t] = halo
        if first:
            halo = halo + halo_of(gather[:, PACK_ROWS + t, :])
        injected.append(lines_both(halo))
        if t == 0:
            inject_ref[0], inject_ref[1] = injected[0]
        if t < STEPS - 1:
            ends = gather[:, t + 1, :]
            for n, (k, side, delta) in enumerate(SPREAD):
                if k <= t + 1:
                    ends = ends + coef_ref[:, STEPS + n, :] * from_line(
                        injected[t + 1 - k][side], delta
                    )


def next_kernel(steps, later, first, peers, axis, ghost, *refs):
    refs = list(refs)

    def take(count):
        taken = refs[:count]
        del refs[:count]
        return taken

    packs = take(peers)
    b_ref, rhs_in, loc_in = take(3)
    coef_ref, add_in, state_in = (None, None, None) if first else take(3)
    last = steps is not None and steps[-1] == 2 * rhs_in.shape[0] - 1
    out_ref = take(1)[0] if last else None
    rhs_ref, add_ref, state_ref = take(3)
    loc_ref, pack_ref = take(2) if later else (None, None)
    coef_out = take(1)[0] if first else None
    gather, halo_ref, inject_ref, *r_refs = refs
    nz = rhs_in.shape[0]
    rows = packs[0].shape[0]
    position = lax.axis_index(axis)

    gather[...] = jnp.zeros(gather.shape, jnp.float32)
    for k in range(peers):
        gather[jnp.bitwise_xor(position, k)] = packs[k][...]
    if first:
        coef_out[...] = gather[:, :PACK_ROWS, :]
    rhs_ref[...] = rhs_in[...]
    if not first:
        add_ref[...] = add_in[...]
    complete_edges(first, gather, gather if first else coef_ref, halo_ref, inject_ref)
    own = pl.ds(position, 1)
    low = low_lanes(HALF)
    row_index = lax.broadcasted_iota(jnp.int32, (HALF, LANES), 0)
    if first:
        for z in range(nz):
            halo_ref[STEPS] = halo_of(gather[:, PACK_ROWS + z, :])
            halo = halo_ref[STEPS, own, :]
            at_edge = jnp.logical_or(
                jnp.logical_and(row_index == 0, low),
                jnp.logical_and(row_index == HALF - 1, jnp.logical_not(low)),
            )
            rhs_ref[z] = rhs_ref[z] + jnp.where(at_edge, halo, 0.0)

    state = None if first else state_in[...]
    for t, step in enumerate(steps):
        z = step if step < nz else 2 * nz - 1 - step
        if state is not None:
            around = sum_y(sum_x(state), halo_ref[t, own, :])
            if step < nz:
                rhs_ref[step - 1] = around - 27.0 * state
        if t == 0:
            left, right = inject_ref[0, own, :], inject_ref[1, own, :]
            state = loc_in[...] + block(b_ref, 0) * left + block(b_ref, LANES - 1) * right
        else:
            (state,) = apply_blocks(b_ref, [rhs_ref[z] + around], r_refs)
            if step >= nz:
                state = state + add_ref[z]
        add_ref[z] = 2.0 * state if step < nz else state
        if step == nz - 1:
            rhs_ref[z] = -27.0 * state
    state_ref[...] = state
    if later:
        pack_ref[...] = jnp.zeros(pack_ref.shape, jnp.float32)
        local_chain(later, b_ref, rhs_ref, add_ref, state, r_refs, pack_ref, loc_ref)
    if last:
        own_lines = HALF - 2 * ghost
        for z in range(nz):
            plane = add_ref[z]
            turned = jnp.concatenate([plane, swap_halves(plane)], axis=0).T
            out_ref[z] = turned[ghost : ghost + own_lines]


def local_kernel(steps, b_ref, rhs_ref, add_ref, state_ref, loc_ref, pack_ref, *r_refs):
    pack_ref[...] = jnp.zeros(pack_ref.shape, jnp.float32)
    local_chain(steps, b_ref, rhs_ref, add_ref, state_ref[...], r_refs, pack_ref, loc_ref)


def finish_kernel(axis, v_ref, *refs):
    parts, out_ref = refs[:-1], refs[-1]
    position = lax.axis_index(axis)
    lines = parts[0].shape[1]
    for k, part in enumerate(parts):
        at = pl.ds(pl.multiple_of(jnp.bitwise_xor(position, k) * lines, lines), lines)
        out_ref[:, at, :] = v_ref[:, at, :] + part[...]


def f32(*shape):
    return jax.ShapeDtypeStruct(shape, jnp.float32)


def call(kernel, ins, outs, scratch, name):
    return pl.pallas_call(
        kernel,
        out_shape=outs,
        in_specs=[VMEM] * len(ins),
        out_specs=[VMEM] * len(outs),
        scratch_shapes=scratch,
        compiler_params=PARAMS,
        name=name,
    )(*ins)


def to_peers(pieces, axis):
    count = lax.axis_size(axis)
    return [pieces[0]] + [
        lax.ppermute(pieces[k], axis, [(i, i ^ k) for i in range(count)]) for k in range(1, count)
    ]


def line_ghosts(cells, dim, width):
    count = lax.axis_size("gx")
    size = cells.shape[dim]
    head = lax.slice_in_dim(cells, 0, width, axis=dim)
    tail = lax.slice_in_dim(cells, size - width, size, axis=dim)
    if count == 2:
        at_first = lax.axis_index("gx") == 0
        other = lax.ppermute(jnp.where(at_first, tail, head), "gx", [(0, 1), (1, 0)])
        zero = jnp.zeros_like(other)
        return jnp.where(at_first, zero, other), jnp.where(at_first, other, zero)
    ups = [(i, i + 1) for i in range(count - 1)]
    downs = [(i + 1, i) for i in range(count - 1)]
    return lax.ppermute(tail, "gx", ups), lax.ppermute(head, "gx", downs)


def block_ghosts(blocks, own, width):
    groups, count = lax.axis_size("gz"), lax.axis_size("gx")
    size = blocks.shape[0]
    reach = -(-width // own)
    assert 2 * reach <= groups
    start = jnp.where(lax.axis_index("gz") < reach, size - width, 0)
    pairs = []
    for g in range(groups):
        for a in range(count - 1):
            if g < reach:
                pairs.append((g * count + a, g * count + a + 1))
            if groups - 1 - g < reach:
                pairs.append((g * count + a + 1, g * count + a))
    return lax.ppermute(lax.dynamic_slice_in_dim(blocks, start, width, 0), ("gz", "gx"), pairs)


def refresh_ghosts(planes, ghost):
    split = planes.reshape(planes.shape[0], HALF, 2, HALF)
    groups, count = lax.axis_size("gz"), lax.axis_size("gx")
    places = [g * count + x for x in range(count) for g in range(groups)]
    ups = list(zip(places[:-1], places[1:]))
    downs = list(zip(places[1:], places[:-1]))
    before = lax.ppermute(split[..., HALF - 2 * ghost : HALF - ghost], ("gz", "gx"), ups)
    after = lax.ppermute(split[..., ghost : 2 * ghost], ("gz", "gx"), downs)
    whole = jnp.concatenate([before, split[..., ghost : HALF - ghost], after], axis=-1)
    return whole.reshape(planes.shape)


def body(initial_field, source_term, block_inverse):
    groups, peers = lax.axis_size("gz"), lax.axis_size("gy")
    nz_local, lines, _ = initial_field.shape
    nz = nz_local * groups
    own = lines // groups
    ghost = (HALF - own) // 2
    assert block_inverse.shape[1:] == (LANES, LANES) and lines % groups == 0
    assert nz % STEPS == 0 and nz <= ghost and peers <= 4
    here = lax.axis_index("gz")

    rows = block_inverse.reshape(lines * LANES, LANES)
    beyond = block_ghosts(block_inverse, own, ghost).reshape(ghost * LANES, LANES)
    blocks = pl.pallas_call(
        functools.partial(layout_kernel, own, "gz"),
        out_shape=f32(LANES * HALF, LANES),
        in_specs=[ANY, ANY],
        out_specs=VMEM,
        scratch_shapes=[
            pltpu.VMEM((HALF * LANES, LANES), jnp.float32),
            pltpu.SemaphoreType.DMA((HALF // math.gcd(own, ghost),)),
        ],
        compiler_params=PARAMS,
        name="layout",
    )(rows, beyond)

    fields = jnp.stack([initial_field, source_term])
    before, after = line_ghosts(fields, 2, ghost)
    wide = jnp.concatenate([before, fields, after], axis=2)
    windows = [
        lax.dynamic_slice_in_dim(wide, jnp.bitwise_xor(here, k) * own, HALF, 2)
        for k in range(groups)
    ]
    fields_here = to_peers(windows, "gz")

    plane = pltpu.VMEM((LANES, LANES), jnp.float32)
    first_rows = PACK_ROWS + 8 * (-(-nz // 8))
    rhs, loc, pack = call(
        functools.partial(first_kernel, "gz", groups),
        [*fields_here, blocks],
        [f32(nz, HALF, LANES), f32(HALF, LANES), f32(first_rows, LANES)],
        [pltpu.VMEM((nz + 2, HALF, LANES), jnp.float32), pltpu.VMEM((nz, HALF, LANES), jnp.float32)]
        + [plane] * 6,
        "first_chain",
    )
    schedule = [list(range(a, a + STEPS)) for a in range(0, 2 * nz, STEPS)]
    coef = add = state = None
    for n, steps in enumerate(schedule):
        first = n == 0
        final = n + 1 == len(schedule)
        renew = steps[-1] == nz - 1 and 2 * nz > ghost
        later = None if final or renew else schedule[n + 1]
        packs = to_peers([pack] * peers, "gy")
        ins = [*packs, blocks, rhs, loc] + ([] if first else [coef, add, state])
        planes = f32(nz, HALF, LANES)
        outs = [f32(nz, own, LANES)] if final else []
        outs += [planes, planes, f32(HALF, LANES)]
        outs += [f32(HALF, LANES), f32(8, LANES)] if later else []
        outs += [f32(8, PACK_ROWS, LANES)] if first else []
        results = call(
            functools.partial(next_kernel, steps, later, first, peers, "gy", ghost),
            ins,
            outs,
            [
                pltpu.VMEM((8, pack.shape[0], LANES), jnp.float32),
                pltpu.VMEM((STEPS + 1, 8, LANES), jnp.float32),
                pltpu.VMEM((2, 8, LANES), jnp.float32),
                plane,
            ],
            "next_chain",
        )
        if final:
            change = results[0]
            break
        rhs, add, state = results[:3]
        if later:
            loc, pack = results[3:5]
        if first:
            coef = results[-1]
        if renew:
            renewed = refresh_ghosts(jnp.concatenate([rhs, add, state[None]]), ghost)
            rhs, add, state = renewed[:nz], renewed[nz : 2 * nz], renewed[2 * nz]
            loc, pack = call(
                functools.partial(local_kernel, schedule[n + 1]),
                [blocks, rhs, add, state],
                [f32(HALF, LANES), f32(8, LANES)],
                [plane],
                "local_chain",
            )

    sends = [
        lax.dynamic_slice_in_dim(change, jnp.bitwise_xor(here, k) * nz_local, nz_local, 0)
        for k in range(groups)
    ]
    parts = to_peers(sends, "gz")
    return call(
        functools.partial(finish_kernel, "gz"),
        [initial_field, *parts],
        [f32(*initial_field.shape)],
        [],
        "finish",
    )[0]


def solution(mesh):
    placed = (P("gz", "gx", "gy"), P("gz", "gx", "gy"), P("gx", "gy", None))
    return jax.shard_map(
        body, mesh=mesh, in_specs=placed, out_specs=P("gz", "gx", "gy"), check_vma=False
    )
```

```python
import functools
import math
import jax
import jax.numpy as jnp
from jax import lax
from jax.experimental import pallas as pl
from jax.experimental.pallas import tpu as pltpu
from jax.sharding import PartitionSpec as P

LANES = 128
HALF = 64
STEPS = 4
SPREAD = [(k, side, delta) for k in range(1, STEPS) for side in range(2) for delta in range(1 - k, k)]
PACK_ROWS = 8 * (-(-(STEPS + len(SPREAD)) // 8))
VMEM = pl.BlockSpec(memory_space=pltpu.VMEM)
HBM = pl.BlockSpec(memory_space=pltpu.HBM)
PARAMS = pltpu.CompilerParams(vmem_limit_bytes=16 * 1024 * 1024)


def low_lanes(rows):
    return lax.broadcasted_iota(jnp.int32, (rows, LANES), 1) < HALF


def swap_halves(a):
    return pltpu.roll(a, HALF, 1)


def from_line(a, delta):
    return a if delta == 0 else pltpu.roll(a, (-delta) % LANES, 1)


def sum_x(a):
    return a + pltpu.roll(a, 1, 1) + pltpu.roll(a, LANES - 1, 1)


def sum_y(a, halo=None):
    low = low_lanes(1)
    first = swap_halves(a[:8])[0:1]
    last = swap_halves(a[HALF - 8 :])[7:8]
    halo = jnp.zeros((1, LANES), jnp.float32) if halo is None else halo
    above = jnp.where(low, halo, last)
    below = jnp.where(low, first, halo)
    row = lax.broadcasted_iota(jnp.int32, a.shape, 0)
    up = jnp.where(row == 0, above, pltpu.roll(a, 1, 0))
    down = jnp.where(row == HALF - 1, below, pltpu.roll(a, HALF - 1, 0))
    return a + up + down


def spread(a):
    low = low_lanes(a.shape[0])
    swapped = swap_halves(a)
    return jnp.where(low, a, swapped), jnp.where(low, swapped, a)


def edges(a):
    return jnp.where(low_lanes(1), a[0:1], a[HALF - 1 : HALF])


def block_column(b_ref, j):
    return b_ref[pl.ds(j, HALF, stride=LANES), :]


def fold_rows(parts):
    row = lax.broadcasted_iota(jnp.int32, (8, LANES), 0)
    for bit in (1, 2, 4):
        first = (row & bit) == 0
        parts = [
            jnp.where(first, a, b) + pltpu.roll(jnp.where(first, b, a), 8 - bit, 0)
            for a, b in zip(parts[::2], parts[1::2])
        ]
    return parts[0]


def apply_blocks(b_ref, rhs, out_ref):
    halves = spread(rhs)
    tiles = [half[8 * t : 8 * t + 8] for half in halves for t in range(HALF // 8)]
    for outer in range(HALF // 8):
        parts = []
        for u in range(8):
            at = (outer * 8 + u) * LANES
            terms = [b_ref[at + 8 * t : at + 8 * t + 8, :] * tiles[t] for t in range(2)]
            for t in range(2, len(tiles)):
                terms[t % 2] = terms[t % 2] + b_ref[at + 8 * t : at + 8 * t + 8, :] * tiles[t]
            parts.append(terms[0] + terms[1])
        out_ref[outer * 8 : outer * 8 + 8, :] = fold_rows(parts)
    return out_ref[...]


def layout_kernel(own, ghost, axis, b_ref, *refs):
    *ghost_refs, out_ref, ready_ref, window, sems = refs
    ready_ref[...] = jnp.zeros(ready_ref.shape, jnp.float32)
    ghost_ref = ghost_refs[0] if ghost_refs else b_ref
    count = b_ref.shape[0] // LANES
    position = lax.axis_index(axis)
    chunk = math.gcd(own, ghost)
    size = chunk * LANES
    copies = []
    for c in range(HALF // chunk):
        start = position * own - ghost + c * chunk
        inside = jnp.logical_and(start >= 0, start < count)
        target = window.at[pl.ds(c * size, size)]
        here = jnp.clip(start, 0, count - chunk)
        beyond = jnp.clip(jnp.where(start < 0, start + ghost, start - count), 0, ghost - chunk)

        @pl.when(inside)
        def _(at=pl.multiple_of(here * LANES, LANES), target=target, c=c):
            pltpu.make_async_copy(b_ref.at[pl.ds(at, size)], target, sems.at[c]).start()

        @pl.when(jnp.logical_not(inside))
        def _(at=pl.multiple_of(beyond * LANES, LANES), target=target, c=c):
            pltpu.make_async_copy(ghost_ref.at[pl.ds(at, size)], target, sems.at[c]).start()

        copies.append(pltpu.make_async_copy(b_ref.at[pl.ds(0, size)], target, sems.at[c]))
    for copy in copies:
        copy.wait()

    def one(outer, carry):
        for u in range(8):
            i = outer * 8 + u
            top = window[pl.ds(i, HALF, stride=LANES), :]
            bottom = window[pl.ds(i + HALF, HALF, stride=LANES), :]
            at = pl.multiple_of(i * LANES, LANES)
            out_ref[pl.ds(at, LANES), :] = jnp.concatenate([top, bottom], axis=0).T
        return carry

    lax.fori_loop(0, HALF // 8, one, 0)


def patch_kernel(axis, groups, b_in, beyond, out_ref):
    ghost = beyond.shape[0] // LANES
    per_turn = HALF // ghost
    unroll = 4
    position = lax.axis_index(axis)
    for place, at in ((0, 0), (groups - 1, HALF - ghost)):

        @pl.when(position == place)
        def _(at=at):
            lane = lax.broadcasted_iota(jnp.int32, (LANES, LANES), 1) % HALF
            mine = jnp.logical_and(lane >= at, lane < at + ghost)

            def one(outer, carry):
                turns = []
                for v in range(unroll):
                    first = (outer * unroll + v) * per_turn
                    rows = [
                        beyond[pl.ds(half * HALF + first + u, ghost, stride=LANES), :]
                        for half in range(2)
                        for u in range(per_turn)
                    ]
                    turns.append(jnp.concatenate(rows, axis=0).T)
                for v in range(unroll):
                    first = (outer * unroll + v) * per_turn
                    for u in range(per_turn):
                        moved = from_line(turns[v], (u * ghost - at) % LANES)
                        here = pl.ds(pl.multiple_of((first + u) * LANES, LANES), LANES)
                        out_ref[here, :] = jnp.where(mine, moved, b_in[here, :])
                return carry

            lax.fori_loop(0, HALF // per_turn // unroll, one, 0)


def responses_kernel(b_ref, pack_ref, r_ref):
    pack_ref[...] = jnp.zeros(pack_ref.shape, jnp.float32)
    low_all = low_lanes(LANES)
    edge_rows = jnp.where(
        low_all,
        b_ref[0:LANES, :],
        b_ref[(HALF - 1) * LANES : HALF * LANES, :],
    )
    firsts = [block_column(b_ref, 0), block_column(b_ref, LANES - 1)]
    shifted = [sum_y(a) for a in firsts]
    plan = [(side, delta) for side in range(2) for delta in (-1, 0, 1)]
    second = {
        (side, delta): apply_blocks(b_ref, from_line(shifted[side], delta), r_ref)
        for side, delta in plan
    }
    for n, (k, side, delta) in enumerate(SPREAD):
        if k == 1:
            row = edges(firsts[side])
        elif k == 2:
            row = edges(second[side, delta])
        else:
            parts = [
                from_line(second[side, delta - m], m) for m in (-1, 0, 1) if abs(delta - m) <= 1
            ]
            top, bottom = spread(sum_y(sum(parts[1:], parts[0])))
            row = jnp.sum(edge_rows[:HALF] * top + edge_rows[HALF:] * bottom, axis=0, keepdims=True)
        pack_ref[pl.ds(STEPS + n, 1), :] = row


def local_chain(steps, b_ref, rhs_ref, add_ref, state, r_ref, pack_ref, first_loc_ref):
    nz = rhs_ref.shape[0]
    if state is not None:
        pack_ref[0:1, :] = edges(state)
    for n, step in enumerate(steps[:-1]):
        z = step if step < nz else 2 * nz - 1 - step
        rhs = rhs_ref[z]
        if state is not None:
            rhs = rhs + sum_y(sum_x(state))
        state = apply_blocks(b_ref, rhs, r_ref)
        if step >= nz:
            state = state + add_ref[z]
        if n == 0:
            first_loc_ref[...] = state
        pack_ref[n + 1 : n + 2, :] = edges(state)


def gather_planes(axis, groups, field_refs, ghost_ref, v_ref, s_ref):
    position = lax.axis_index(axis)
    low = low_lanes(HALF)
    nz_local = field_refs[0].shape[1]
    for k, ref in enumerate(field_refs):
        base = jnp.bitwise_xor(position, k) * nz_local
        for p in range(nz_local):
            for kind, target in ((0, v_ref), (1, s_ref)):
                plane = ref[kind, p]
                if ghost_ref is not None:
                    beyond = ghost_ref[(groups - 1) ^ k, kind, p]
                    ghost = beyond.shape[0]
                    first = jnp.where(position == 0, beyond, plane[:ghost])
                    last = jnp.where(position == groups - 1, beyond, plane[HALF - ghost :])
                    plane = jnp.concatenate([first, plane[ghost : HALF - ghost], last], axis=0)
                turned = jnp.concatenate([plane, plane], axis=0).T
                target[base + p + 1 - kind] = jnp.where(low, turned[:HALF], turned[HALF:])


def first_kernel(axis, fields, late, *refs):
    field_refs = refs[:fields]
    ghost_ref = refs[fields] if late else None
    refs = refs[1:] if late else refs
    b_ref, answers_ref, rhs_ref, loc_ref, pack_ref, v_ref, s_ref, r_ref = refs[fields:]
    nz = rhs_ref.shape[0]
    pack_ref[...] = jnp.zeros(pack_ref.shape, jnp.float32)
    pack_ref[:PACK_ROWS, :] = answers_ref[...]
    v_ref[0] = jnp.zeros((HALF, LANES), jnp.float32)
    v_ref[nz + 1] = jnp.zeros((HALF, LANES), jnp.float32)
    gather_planes(axis, fields, field_refs, ghost_ref, v_ref, s_ref)
    for z in range(nz):
        around = v_ref[z] + v_ref[z + 1] + v_ref[z + 2]
        rhs_ref[z] = s_ref[z] - 27.0 * v_ref[z + 1] + sum_y(sum_x(around))
        pack_ref[PACK_ROWS + z : PACK_ROWS + z + 1, :] = edges(around)
    local_chain(list(range(STEPS)), b_ref, rhs_ref, None, None, r_ref, pack_ref, loc_ref)


def halo_of(ends):
    swapped = swap_halves(ends)
    return sum_x(jnp.where(low_lanes(8), pltpu.roll(swapped, 1, 0), pltpu.roll(swapped, 7, 0)))


def lines_both(row):
    swapped = swap_halves(row)
    low = low_lanes(8)
    return jnp.where(low, row, swapped), jnp.where(low, swapped, row)


def complete_edges(first, gather, coef_ref, halo_ref, inject_ref):
    injected = []
    ends = None if first else gather[:, 0, :]
    for t in range(STEPS):
        halo = jnp.zeros((8, LANES), jnp.float32) if ends is None else halo_of(ends)
        halo_ref[t] = halo
        if first:
            halo = halo + halo_of(gather[:, PACK_ROWS + t, :])
        injected.append(lines_both(halo))
        if t == 0:
            inject_ref[0], inject_ref[1] = injected[0]
        if t < STEPS - 1:
            ends = gather[:, t + 1, :]
            for n, (k, side, delta) in enumerate(SPREAD):
                if k <= t + 1:
                    ends = ends + coef_ref[:, STEPS + n, :] * from_line(
                        injected[t + 1 - k][side], delta
                    )


def ghost_pack_kernel(axis, own, ghost, *refs):
    *window_refs, ready_ref, out_ref = refs
    at = jnp.where(lax.axis_index(axis) == 0, ghost, own)
    for k, ref in enumerate(window_refs):
        out_ref[k] = ref[:, :, pl.ds(pl.multiple_of(at, 8), ghost), :]


def next_kernel(steps, later, first, peers, axis, ghost, *refs):
    refs = list(refs)

    def take(count):
        taken = refs[:count]
        del refs[:count]
        return taken

    packs = take(peers)
    b_ref, rhs_in, loc_in = take(3)
    coef_ref, add_in, state_in = (None, None, None) if first else take(3)
    last = steps is not None and steps[-1] == 2 * rhs_in.shape[0] - 1
    out_ref = take(1)[0] if last else None
    rhs_ref, add_ref, state_ref = take(3)
    loc_ref, pack_ref = take(2) if later else (None, None)
    coef_out = take(1)[0] if first else None
    gather, halo_ref, inject_ref, r_ref = refs
    nz = rhs_in.shape[0]
    rows = packs[0].shape[0]
    position = lax.axis_index(axis)

    gather[...] = jnp.zeros(gather.shape, jnp.float32)
    for k in range(peers):
        gather[jnp.bitwise_xor(position, k)] = packs[k][...]
    if first:
        coef_out[...] = gather[:, :PACK_ROWS, :]
    rhs_ref[...] = rhs_in[...]
    if not first:
        add_ref[...] = add_in[...]
    complete_edges(first, gather, gather if first else coef_ref, halo_ref, inject_ref)
    own = pl.ds(position, 1)
    low = low_lanes(HALF)
    row_index = lax.broadcasted_iota(jnp.int32, (HALF, LANES), 0)
    if first:
        for z in range(nz):
            halo_ref[STEPS] = halo_of(gather[:, PACK_ROWS + z, :])
            halo = halo_ref[STEPS, own, :]
            at_edge = jnp.logical_or(
                jnp.logical_and(row_index == 0, low),
                jnp.logical_and(row_index == HALF - 1, jnp.logical_not(low)),
            )
            rhs_ref[z] = rhs_ref[z] + jnp.where(at_edge, halo, 0.0)

    state = None if first else state_in[...]
    for t, step in enumerate(steps):
        z = step if step < nz else 2 * nz - 1 - step
        if state is not None:
            around = sum_y(sum_x(state), halo_ref[t, own, :])
            if step < nz:
                rhs_ref[step - 1] = around - 27.0 * state
        if t == 0:
            left, right = inject_ref[0, own, :], inject_ref[1, own, :]
            state = (
                loc_in[...] + block_column(b_ref, 0) * left + block_column(b_ref, LANES - 1) * right
            )
        else:
            state = apply_blocks(b_ref, rhs_ref[z] + around, r_ref)
            if step >= nz:
                state = state + add_ref[z]
        add_ref[z] = 2.0 * state if step < nz else state
        if step == nz - 1:
            rhs_ref[z] = -27.0 * state
    state_ref[...] = state
    if later:
        pack_ref[...] = jnp.zeros(pack_ref.shape, jnp.float32)
        local_chain(later, b_ref, rhs_ref, add_ref, state, r_ref, pack_ref, loc_ref)
    if last:
        own_lines = HALF - 2 * ghost
        for z in range(nz):
            plane = add_ref[z]
            turned = jnp.concatenate([plane, swap_halves(plane)], axis=0).T
            out_ref[z] = turned[ghost : ghost + own_lines]


def local_kernel(steps, b_ref, rhs_ref, add_ref, state_ref, loc_ref, pack_ref, r_ref):
    pack_ref[...] = jnp.zeros(pack_ref.shape, jnp.float32)
    local_chain(steps, b_ref, rhs_ref, add_ref, state_ref[...], r_ref, pack_ref, loc_ref)


def finish_kernel(axis, v_ref, *refs):
    parts, out_ref = refs[:-1], refs[-1]
    position = lax.axis_index(axis)
    lines = parts[0].shape[1]
    for k, part in enumerate(parts):
        at = pl.ds(pl.multiple_of(jnp.bitwise_xor(position, k) * lines, lines), lines)
        out_ref[:, at, :] = v_ref[:, at, :] + part[...]


def f32(*shape):
    return jax.ShapeDtypeStruct(shape, jnp.float32)


def call(kernel, ins, outs, scratch, name):
    return pl.pallas_call(
        kernel,
        out_shape=outs,
        in_specs=[VMEM] * len(ins),
        out_specs=[VMEM] * len(outs),
        scratch_shapes=scratch,
        compiler_params=PARAMS,
        name=name,
    )(*ins)


def in_hbm(a):
    return pltpu.with_memory_space_constraint(a, pltpu.HBM)


def to_peers(pieces, axis):
    count = lax.axis_size(axis)
    got = {0: pieces[0]}
    for k in reversed(range(1, count)):
        got[k] = lax.ppermute(pieces[k], axis, [(i, i ^ k) for i in range(count)])
    return [got[k] for k in range(count)]


def line_ghosts(cells, dim, width):
    count = lax.axis_size("gx")
    size = cells.shape[dim]
    head = lax.slice_in_dim(cells, 0, width, axis=dim)
    tail = lax.slice_in_dim(cells, size - width, size, axis=dim)
    if count == 2:
        at_first = lax.axis_index("gx") == 0
        other = lax.ppermute(jnp.where(at_first, tail, head), "gx", [(0, 1), (1, 0)])
        zero = jnp.zeros_like(other)
        return jnp.where(at_first, zero, other), jnp.where(at_first, other, zero)
    ups = [(i, i + 1) for i in range(count - 1)]
    downs = [(i + 1, i) for i in range(count - 1)]
    return lax.ppermute(tail, "gx", ups), lax.ppermute(head, "gx", downs)


def block_ghosts(blocks, own, width):
    groups, count = lax.axis_size("gz"), lax.axis_size("gx")
    size = blocks.shape[0]
    reach = -(-width // own)
    assert 2 * reach <= groups
    shift = reach if 4 * reach <= groups else 0
    start = jnp.where(lax.axis_index("gz") < groups // 2, size - width, 0)
    pairs = []
    for g in range(reach):
        for a in range(count - 1):
            pairs.append(((g + shift) * count + a, g * count + a + 1))
            pairs.append(((groups - 1 - g - shift) * count + a + 1, (groups - 1 - g) * count + a))
    return lax.ppermute(lax.dynamic_slice_in_dim(blocks, start, width, 0), ("gz", "gx"), pairs)


def window_ghosts(windows, ready, own, ghost):
    groups, count = lax.axis_size("gz"), lax.axis_size("gx")
    nz_local = windows[0].shape[1]
    (lines,) = call(
        functools.partial(ghost_pack_kernel, "gz", own, ghost),
        [*windows, ready],
        [f32(groups, 2, nz_local, ghost, LANES)],
        [],
        "ghost_pack",
    )
    end = (groups - 1) * count
    pairs = [(end + a, a + 1) for a in range(count - 1)]
    pairs += [(a + 1, end + a) for a in range(count - 1)]
    return lax.ppermute(lines, ("gz", "gx"), pairs)


def refresh_ghosts(planes, ghost):
    split = planes.reshape(planes.shape[0], HALF, 2, HALF)
    groups, count = lax.axis_size("gz"), lax.axis_size("gx")
    places = [g * count + x for x in range(count) for g in range(groups)]
    ups = list(zip(places[:-1], places[1:]))
    downs = list(zip(places[1:], places[:-1]))
    before = lax.ppermute(split[..., HALF - 2 * ghost : HALF - ghost], ("gz", "gx"), ups)
    after = lax.ppermute(split[..., ghost : 2 * ghost], ("gz", "gx"), downs)
    whole = jnp.concatenate([before, split[..., ghost : HALF - ghost], after], axis=-1)
    return whole.reshape(planes.shape)


def body(initial_field, source_term, block_inverse):
    groups, peers = lax.axis_size("gz"), lax.axis_size("gy")
    nz_local, lines, _ = initial_field.shape
    nz = nz_local * groups
    own = lines // groups
    ghost = (HALF - own) // 2
    assert block_inverse.shape[1:] == (LANES, LANES) and lines % groups == 0
    assert nz % STEPS == 0 and nz <= ghost and peers <= 4
    here = lax.axis_index("gz")

    fields = jnp.stack([initial_field, source_term])
    rows = block_inverse.reshape(lines * LANES, LANES)
    beyond = block_ghosts(block_inverse, own, ghost).reshape(ghost * LANES, LANES)
    late = own == 2 * ghost
    turned = LANES * HALF * LANES * 4
    blocks, ready = pl.pallas_call(
        functools.partial(layout_kernel, own, ghost, "gz"),
        out_shape=[f32(LANES * HALF, LANES), f32(8, LANES)],
        in_specs=[HBM] * (1 if late else 2),
        out_specs=[VMEM, VMEM],
        scratch_shapes=[
            pltpu.VMEM((HALF * LANES, LANES), jnp.float32),
            pltpu.SemaphoreType.DMA((HALF // math.gcd(own, ghost),)),
        ],
        compiler_params=PARAMS,
        cost_estimate=pl.CostEstimate(flops=0, bytes_accessed=4 * turned, transcendentals=0),
        name="layout",
    )(*[in_hbm(a) for a in ([rows] if late else [rows, beyond])])
    if late:
        wide = jnp.pad(fields, ((0, 0), (0, 0), (ghost, ghost), (0, 0)))
    else:
        before, after = line_ghosts(fields, 2, ghost)
        wide = jnp.concatenate([before, fields, after], axis=2)
    windows = [
        lax.dynamic_slice_in_dim(wide, jnp.bitwise_xor(here, k) * own, HALF, 2)
        for k in range(groups)
    ]
    fields_here = to_peers(windows, "gz")
    ghosts_here = []
    if late:
        ghosts_here = [window_ghosts(fields_here, ready, own, ghost)]
        blocks = pl.pallas_call(
            functools.partial(patch_kernel, "gz", groups),
            out_shape=f32(LANES * HALF, LANES),
            in_specs=[VMEM, VMEM],
            out_specs=VMEM,
            input_output_aliases={0: 0},
            compiler_params=PARAMS,
            name="patch",
        )(blocks, beyond)


    plane = pltpu.VMEM((HALF, LANES), jnp.float32)
    (answers,) = call(
        responses_kernel, [blocks], [f32(PACK_ROWS, LANES)], [plane], "responses"
    )
    first_rows = PACK_ROWS + 8 * (-(-nz // 8))
    rhs, loc, pack = call(
        functools.partial(first_kernel, "gz", groups, late),
        [*fields_here, *ghosts_here, blocks, answers],
        [f32(nz, HALF, LANES), f32(HALF, LANES), f32(first_rows, LANES)],
        [pltpu.VMEM((nz + 2, HALF, LANES), jnp.float32), pltpu.VMEM((nz, HALF, LANES), jnp.float32)]
        + [plane],
        "first_chain",
    )
    schedule = [list(range(a, a + STEPS)) for a in range(0, 2 * nz, STEPS)]
    coef = add = state = None
    for n, steps in enumerate(schedule):
        first = n == 0
        final = n + 1 == len(schedule)
        renew = steps[-1] == nz - 1 and 2 * nz > ghost
        later = None if final or renew else schedule[n + 1]
        packs = to_peers([pack] * peers, "gy")
        ins = [*packs, blocks, rhs, loc] + ([] if first else [coef, add, state])
        planes = f32(nz, HALF, LANES)
        outs = [f32(nz, own, LANES)] if final else []
        outs += [planes, planes, f32(HALF, LANES)]
        outs += [f32(HALF, LANES), f32(8, LANES)] if later else []
        outs += [f32(8, PACK_ROWS, LANES)] if first else []
        results = call(
            functools.partial(next_kernel, steps, later, first, peers, "gy", ghost),
            ins,
            outs,
            [
                pltpu.VMEM((8, pack.shape[0], LANES), jnp.float32),
                pltpu.VMEM((STEPS + 1, 8, LANES), jnp.float32),
                pltpu.VMEM((2, 8, LANES), jnp.float32),
                plane,
            ],
            "next_chain",
        )
        if final:
            change = results[0]
            break
        rhs, add, state = results[:3]
        if later:
            loc, pack = results[3:5]
        if first:
            coef = results[-1]
        if renew:
            renewed = refresh_ghosts(jnp.concatenate([rhs, add, state[None]]), ghost)
            rhs, add, state = renewed[:nz], renewed[nz : 2 * nz], renewed[2 * nz]
            loc, pack = call(
                functools.partial(local_kernel, schedule[n + 1]),
                [blocks, rhs, add, state],
                [f32(HALF, LANES), f32(8, LANES)],
                [plane],
                "local_chain",
            )

    sends = [
        lax.dynamic_slice_in_dim(change, jnp.bitwise_xor(here, k) * nz_local, nz_local, 0)
        for k in range(groups)
    ]
    parts = to_peers(sends, "gz")
    return call(
        functools.partial(finish_kernel, "gz"),
        [initial_field, *parts],
        [f32(*initial_field.shape)],
        [],
        "finish",
    )[0]


def solution(mesh):
    placed = (P("gz", "gx", "gy"), P("gz", "gx", "gy"), P("gx", "gy", None))
    return jax.shard_map(
        body, mesh=mesh, in_specs=placed, out_specs=P("gz", "gx", "gy"), check_vma=False
    )
```

```python
import functools
import math
import jax
import jax.numpy as jnp
from jax import lax
from jax.experimental import pallas as pl
from jax.experimental.pallas import tpu as pltpu
from jax.sharding import PartitionSpec as P

LANES = 128
HALF = 64
STEPS = 4
SPREAD = [(k, side, delta) for k in range(1, STEPS) for side in range(2) for delta in range(1 - k, k)]
PLANES = sum(k <= 2 for k, _, _ in SPREAD)
PACK_ROWS = 8 * (-(-(STEPS + len(SPREAD)) // 8))
VMEM = pl.BlockSpec(memory_space=pltpu.VMEM)
HBM = pl.BlockSpec(memory_space=pltpu.HBM)
PARAMS = pltpu.CompilerParams(vmem_limit_bytes=16 * 1024 * 1024)


def low_lanes(rows):
    return lax.broadcasted_iota(jnp.int32, (rows, LANES), 1) < HALF


def swap_halves(a):
    return pltpu.roll(a, HALF, 1)


def from_line(a, delta):
    return a if delta == 0 else pltpu.roll(a, (-delta) % LANES, 1)


def sum_x(a):
    return a + pltpu.roll(a, 1, 1) + pltpu.roll(a, LANES - 1, 1)


def sum_y(a, halo=None):
    low = low_lanes(1)
    first = swap_halves(a[:8])[0:1]
    last = swap_halves(a[HALF - 8 :])[7:8]
    halo = jnp.zeros((1, LANES), jnp.float32) if halo is None else halo
    above = jnp.where(low, halo, last)
    below = jnp.where(low, first, halo)
    row = lax.broadcasted_iota(jnp.int32, a.shape, 0)
    up = jnp.where(row == 0, above, pltpu.roll(a, 1, 0))
    down = jnp.where(row == HALF - 1, below, pltpu.roll(a, HALF - 1, 0))
    return a + up + down


def spread(a):
    low = low_lanes(a.shape[0])
    swapped = swap_halves(a)
    return jnp.where(low, a, swapped), jnp.where(low, swapped, a)


def edges(a):
    return jnp.where(low_lanes(1), a[0:1], a[HALF - 1 : HALF])


def block_column(b_ref, j):
    return b_ref[pl.ds(j, HALF, stride=LANES), :]


def fold_rows(parts):
    row = lax.broadcasted_iota(jnp.int32, (8, LANES), 0)
    for bit in (1, 2, 4):
        first = (row & bit) == 0
        parts = [
            jnp.where(first, a, b) + pltpu.roll(jnp.where(first, b, a), 8 - bit, 0)
            for a, b in zip(parts[::2], parts[1::2])
        ]
    return parts[0]


def apply_blocks(b_ref, rhs, out_ref):
    tiles = [half[8 * t : 8 * t + 8] for half in spread(rhs) for t in range(HALF // 8)]

    def rows(outer, carry):
        parts = []
        for u in range(8):
            at = (outer * 8 + u) * LANES
            terms = [b_ref[pl.ds(at + 8 * t, 8), :] * tiles[t] for t in range(2)]
            for t in range(2, len(tiles)):
                terms[t % 2] = terms[t % 2] + b_ref[pl.ds(at + 8 * t, 8), :] * tiles[t]
            parts.append(terms[0] + terms[1])
        out_ref[pl.ds(outer * 8, 8), :] = fold_rows(parts)
        return carry

    lax.fori_loop(0, HALF // 8, rows, 0, unroll=True)
    return out_ref[...]


def edge_rows(b_ref):
    return jnp.where(
        low_lanes(LANES), b_ref[0:LANES, :], b_ref[(HALF - 1) * LANES : HALF * LANES, :]
    )


def apply_edges(rows, rhs):
    top, bottom = spread(rhs)
    return jnp.sum(rows[:HALF] * top + rows[HALF:] * bottom, axis=0, keepdims=True)


def layout_kernel(own, ghost, axis, b_ref, *refs):
    *ghost_refs, out_ref, ready_ref, window, sems = refs
    ready_ref[...] = jnp.zeros(ready_ref.shape, jnp.float32)
    ghost_ref = ghost_refs[0] if ghost_refs else b_ref
    count = b_ref.shape[0] // LANES
    position = lax.axis_index(axis)
    chunk = math.gcd(own, ghost)
    size = chunk * LANES
    copies = []
    for c in range(HALF // chunk):
        start = position * own - ghost + c * chunk
        inside = jnp.logical_and(start >= 0, start < count)
        target = window.at[pl.ds(c * size, size)]
        here = jnp.clip(start, 0, count - chunk)
        beyond = jnp.clip(jnp.where(start < 0, start + ghost, start - count), 0, ghost - chunk)

        @pl.when(inside)
        def _(at=pl.multiple_of(here * LANES, LANES), target=target, c=c):
            pltpu.make_async_copy(b_ref.at[pl.ds(at, size)], target, sems.at[c]).start()

        @pl.when(jnp.logical_not(inside))
        def _(at=pl.multiple_of(beyond * LANES, LANES), target=target, c=c):
            pltpu.make_async_copy(ghost_ref.at[pl.ds(at, size)], target, sems.at[c]).start()

        copies.append(pltpu.make_async_copy(b_ref.at[pl.ds(0, size)], target, sems.at[c]))
    for copy in copies:
        copy.wait()

    def one(outer, carry):
        for u in range(8):
            i = outer * 8 + u
            top = window[pl.ds(i, HALF, stride=LANES), :]
            bottom = window[pl.ds(i + HALF, HALF, stride=LANES), :]
            at = pl.multiple_of(i * LANES, LANES)
            out_ref[pl.ds(at, LANES), :] = jnp.concatenate([top, bottom], axis=0).T
        return carry

    lax.fori_loop(0, HALF // 8, one, 0)


def tail_kernel(axis, groups, b_ref, tail_ref, sems):
    ghost = tail_ref.shape[0]
    start = jnp.where(lax.axis_index(axis) < groups // 2, b_ref.shape[0] - ghost, 0)
    part = ghost // 4
    copies = [
        pltpu.make_async_copy(
            b_ref.at[pl.ds(start + n * part, part)], tail_ref.at[pl.ds(n * part, part)], sems.at[n]
        )
        for n in range(4)
    ]
    for copy in copies:
        copy.start()
    for copy in copies:
        copy.wait()


def pack_kernel(axis, own, ghost, v_ref, s_ref, *refs):
    *window_refs, sems = refs
    position = lax.axis_index(axis)
    last = v_ref.shape[1] - ghost
    copies = []
    for k, window_ref in enumerate(window_refs):
        peer = jnp.bitwise_xor(position, k)
        for c in range(HALF // ghost):
            at = pl.multiple_of(jnp.clip(peer * own - ghost + c * ghost, 0, last), ghost)
            for kind, ref in enumerate((v_ref, s_ref)):
                copies.append(
                    pltpu.make_async_copy(
                        ref.at[:, pl.ds(at, ghost), :],
                        window_ref.at[kind, :, pl.ds(c * ghost, ghost), :],
                        sems.at[len(copies)],
                    )
                )
    for copy in copies:
        copy.start()
    for copy in copies:
        copy.wait()


def patch_kernel(axis, groups, b_in, beyond, out_ref):
    ghost = beyond.shape[0] // LANES
    per_turn = HALF // ghost
    unroll = 4
    position = lax.axis_index(axis)
    for place, at in ((0, 0), (groups - 1, HALF - ghost)):

        @pl.when(position == place)
        def _(at=at):
            lane = lax.broadcasted_iota(jnp.int32, (LANES, LANES), 1) % HALF
            mine = jnp.logical_and(lane >= at, lane < at + ghost)

            def one(outer, carry):
                turns = []
                for v in range(unroll):
                    first = (outer * unroll + v) * per_turn
                    rows = [
                        beyond[pl.ds(half * HALF + first + u, ghost, stride=LANES), :]
                        for half in range(2)
                        for u in range(per_turn)
                    ]
                    turns.append(jnp.concatenate(rows, axis=0).T)
                for v in range(unroll):
                    first = (outer * unroll + v) * per_turn
                    for u in range(per_turn):
                        moved = from_line(turns[v], (u * ghost - at) % LANES)
                        here = pl.ds(pl.multiple_of((first + u) * LANES, LANES), LANES)
                        out_ref[here, :] = jnp.where(mine, moved, b_in[here, :])
                return carry

            lax.fori_loop(0, HALF // per_turn // unroll, one, 0)


def responses_kernel(b_ref, pack_ref, plane_ref, r_ref, many_ref):
    pack_ref[...] = jnp.zeros(pack_ref.shape, jnp.float32)
    firsts = [block_column(b_ref, 0), block_column(b_ref, LANES - 1)]
    for side, first in enumerate(firsts):
        many_ref[side] = first
        shifted = sum_y(first)
        for n, (k, at_side, delta) in enumerate(SPREAD):
            if k == 2 and at_side == side:
                many_ref[n] = from_line(shifted, delta)

    def product(n, carry):
        many_ref[n] = apply_blocks(b_ref, many_ref[n], r_ref)
        return carry

    lax.fori_loop(2, PLANES, product, 0, unroll=True)
    second = {SPREAD[n][1:]: many_ref[n] for n in range(2, PLANES)}
    rows = edge_rows(b_ref)
    for n, (k, side, delta) in enumerate(SPREAD):
        if k <= 2:
            row = edges(many_ref[n])
        else:
            parts = [
                from_line(second[side, delta - m], m) for m in (-1, 0, 1) if abs(delta - m) <= 1
            ]
            row = apply_edges(rows, sum_y(sum(parts[1:], parts[0])))
        pack_ref[pl.ds(STEPS + n, 1), :] = row
    plane_ref[...] = many_ref[...]


def planes_of(steps, nz):
    return (steps[0], 1) if steps[0] < nz else (2 * nz - 1 - steps[0], -1)


def local_chain(steps, b_ref, rhs_ref, add_ref, state, r_ref, pack_ref, loc_ref):
    first, move = planes_of(steps, rhs_ref.shape[0])
    if state is None:
        state = jnp.zeros((HALF, LANES), jnp.float32)
    else:
        pack_ref[0:1, :] = edges(state)
    ahead = len(steps) - 2

    def transition(n, state):
        z = first + move * n
        state = apply_blocks(b_ref, rhs_ref[z] + sum_y(sum_x(state)), r_ref)
        if move < 0:
            state = state + add_ref[z]
        loc_ref[n] = state
        pack_ref[pl.ds(n + 1, 1), :] = edges(state)
        return state

    state = lax.fori_loop(0, ahead, transition, state, unroll=True)
    z = first + move * ahead
    row = apply_edges(edge_rows(b_ref), rhs_ref[z] + sum_y(sum_x(state)))
    pack_ref[ahead + 1 : ahead + 2, :] = row + edges(add_ref[z]) if move < 0 else row


def copy_pack(pack_refs):
    first = pack_refs[0][...]
    for ref in pack_refs[1:]:
        ref[: first.shape[0], :] = first
        ref[first.shape[0] :, :] = jnp.zeros((ref.shape[0] - first.shape[0], LANES), jnp.float32)


def gather_planes(axis, groups, field_refs, ghost_ref, v_ref, s_ref):
    position = lax.axis_index(axis)
    low = low_lanes(HALF)
    nz_local = field_refs[0].shape[1]
    for k, ref in enumerate(field_refs):
        base = jnp.bitwise_xor(position, k) * nz_local
        for p in range(nz_local):
            for kind, target in ((0, v_ref), (1, s_ref)):
                plane = ref[kind, p]
                if ghost_ref is not None:
                    beyond = ghost_ref[(groups - 1) ^ k, kind, p]
                    ghost = beyond.shape[0]
                    first = jnp.where(position == 0, beyond, plane[:ghost])
                    last = jnp.where(position == groups - 1, beyond, plane[HALF - ghost :])
                    plane = jnp.concatenate([first, plane[ghost : HALF - ghost], last], axis=0)
                turned = jnp.concatenate([plane, plane], axis=0).T
                target[base + p + 1 - kind] = jnp.where(low, turned[:HALF], turned[HALF:])


def first_kernel(axis, fields, late, *refs):
    field_refs = refs[:fields]
    ghost_ref = refs[fields] if late else None
    refs = refs[1:] if late else refs
    b_ref, answers_ref, rhs_ref, loc_ref, *pack_refs, v_ref, s_ref, r_ref = refs[fields:]
    pack_ref = pack_refs[0]
    nz = rhs_ref.shape[0]
    pack_ref[...] = jnp.zeros(pack_ref.shape, jnp.float32)
    pack_ref[:PACK_ROWS, :] = answers_ref[...]
    v_ref[0] = jnp.zeros((HALF, LANES), jnp.float32)
    v_ref[nz + 1] = jnp.zeros((HALF, LANES), jnp.float32)
    gather_planes(axis, fields, field_refs, ghost_ref, v_ref, s_ref)
    for z in range(nz):
        around = v_ref[z] + v_ref[z + 1] + v_ref[z + 2]
        rhs_ref[z] = s_ref[z] - 27.0 * v_ref[z + 1] + sum_y(sum_x(around))
        pack_ref[PACK_ROWS + z : PACK_ROWS + z + 1, :] = edges(around)
    local_chain(list(range(STEPS)), b_ref, rhs_ref, None, None, r_ref, pack_ref, loc_ref)
    copy_pack(pack_refs)


def beside(ends, swapped):
    low = low_lanes(8)
    left = pltpu.roll(jnp.where(low, swapped, ends), 1, 0)
    right = pltpu.roll(jnp.where(low, ends, swapped), 7, 0)
    return left, right


def complete_edges(first, gather, coef_ref, halo_ref, inject_ref):
    low = low_lanes(8)
    known = [gather[:, t, :] for t in range(STEPS)]
    totals = [(row, swap_halves(row)) for row in known]
    for t in range(STEPS):
        halo = None if first and t == 0 else beside(*totals[t])
        if halo is None:
            halo_ref[t] = jnp.zeros((8, LANES), jnp.float32)
        else:
            halo_ref[t] = sum_x(jnp.where(low, *halo))
        if first:
            row = gather[:, PACK_ROWS + t, :]
            start = beside(row, swap_halves(row))
            halo = start if halo is None else [x + y for x, y in zip(halo, start)]
        reach = STEPS - 1 - t
        width = max(reach - 1, 1 if t == 0 else 0)
        if reach < 1:
            break
        summed = []
        for cells in halo:
            moved = {m: from_line(cells, m) for m in range(-width - 1, width + 2)}
            summed.append(
                {m: moved[m - 1] + moved[m] + moved[m + 1] for m in range(-width, width + 1)}
            )
        for n, (k, side, delta) in enumerate(SPREAD):
            if k <= reach:
                coef = coef_ref[:, STEPS + n, :]
                ends, swapped = totals[t + k]
                totals[t + k] = (
                    ends + coef * summed[side][delta],
                    swapped + swap_halves(coef) * summed[side][delta],
                )
        if t < 2:
            for n, (k, side, delta) in enumerate(SPREAD[: PLANES if t == 0 else 2]):
                inject_ref[t * PLANES + n] = summed[side][delta]


def ghost_pack_kernel(axis, own, ghost, *refs):
    *window_refs, ready_ref, out_ref = refs
    at = jnp.where(lax.axis_index(axis) == 0, ghost, own)
    for k, ref in enumerate(window_refs):
        out_ref[k] = ref[:, :, pl.ds(pl.multiple_of(at, 8), ghost), :]


def next_kernel(steps, later, first, peers, axis, ghost, *refs):
    refs = list(refs)

    def take(count):
        taken = refs[:count]
        del refs[:count]
        return taken

    packs = take(peers)
    b_ref, plane_ref, rhs_in, loc_in = take(4)
    coef_ref, add_in, state_in = (None, None, None) if first else take(3)
    last = steps is not None and steps[-1] == 2 * rhs_in.shape[0] - 1
    out_ref = take(1)[0] if last else None
    rhs_ref, add_ref, state_ref = take(3)
    loc_ref, *pack_refs = take(peers) if later else (None,)
    coef_out = take(1)[0] if first else None
    gather, halo_ref, inject_ref, r_ref = refs
    nz = rhs_in.shape[0]
    position = lax.axis_index(axis)

    gather[...] = jnp.zeros(gather.shape, jnp.float32)
    for k in range(peers):
        gather[jnp.bitwise_xor(position, k)] = packs[k][: gather.shape[1], :]
    if first:
        coef_out[...] = gather[:, :PACK_ROWS, :]
    complete_edges(first, gather, gather if first else coef_ref, halo_ref, inject_ref)
    own = pl.ds(position, 1)
    low = low_lanes(HALF)
    row_index = lax.broadcasted_iota(jnp.int32, (HALF, LANES), 0)
    if first:
        for z in range(nz):
            row = gather[:, PACK_ROWS + z, :]
            left, right = beside(row, swap_halves(row))
            halo_ref[STEPS + z] = sum_x(jnp.where(low_lanes(8), left, right))
            halo = halo_ref[STEPS + z, own, :]
            at_edge = jnp.logical_or(
                jnp.logical_and(row_index == 0, low),
                jnp.logical_and(row_index == HALF - 1, jnp.logical_not(low)),
            )
            rhs_ref[z] = rhs_ref[z] + jnp.where(at_edge, halo, 0.0)

    first_plane, move = planes_of(steps, nz)

    def keep(z, state):
        add_ref[z] = 2.0 * state if move > 0 else state

    if not first:
        state = state_in[...]
        if move > 0:
            around = sum_y(sum_x(state), halo_ref[0, own, :])
            rhs_ref[first_plane - 1] = around - 27.0 * state
    state = loc_in[0]
    for n in range(2):
        state = state + plane_ref[n] * inject_ref[n, own, :]
    keep(first_plane, state)
    if move > 0:
        rhs_ref[first_plane] = sum_y(sum_x(state), halo_ref[1, own, :]) - 27.0 * state
    state = loc_in[1]
    for n in range(PLANES):
        state = state + plane_ref[n] * inject_ref[n if n >= 2 else PLANES + n, own, :]
    keep(first_plane + move, state)

    def transition(t, state):
        z = first_plane + move * t
        around = sum_y(sum_x(state), halo_ref[t, own, :])
        if move > 0:
            rhs_ref[z - 1] = around - 27.0 * state
        state = apply_blocks(b_ref, rhs_ref[z] + around, r_ref)
        if move < 0:
            state = state + add_ref[z]
        keep(z, state)
        return state

    state = lax.fori_loop(2, STEPS, transition, state, unroll=True)
    if steps[-1] == nz - 1:
        rhs_ref[nz - 1] = -27.0 * state
    state_ref[...] = state
    if later:
        pack_ref = pack_refs[0]
        pack_ref[...] = jnp.zeros(pack_ref.shape, jnp.float32)
        local_chain(later, b_ref, rhs_ref, add_ref, state, r_ref, pack_ref, loc_ref)
        copy_pack(pack_refs)
    if last:
        own_lines = HALF - 2 * ghost
        for z in range(nz):
            plane = add_ref[z]
            turned = jnp.concatenate([plane, swap_halves(plane)], axis=0).T
            out_ref[z] = turned[ghost : ghost + own_lines]


def local_kernel(steps, b_ref, rhs_ref, add_ref, state_ref, loc_ref, *refs):
    *pack_refs, r_ref = refs
    pack_refs[0][...] = jnp.zeros(pack_refs[0].shape, jnp.float32)
    local_chain(steps, b_ref, rhs_ref, add_ref, state_ref[...], r_ref, pack_refs[0], loc_ref)
    copy_pack(pack_refs)


def finish_kernel(axis, v_ref, *refs):
    parts, out_ref = refs[:-1], refs[-1]
    position = lax.axis_index(axis)
    lines = parts[0].shape[1]
    for k, part in enumerate(parts):
        at = pl.ds(pl.multiple_of(jnp.bitwise_xor(position, k) * lines, lines), lines)
        out_ref[:, at, :] = v_ref[:, at, :] + part[...]


def f32(*shape):
    return jax.ShapeDtypeStruct(shape, jnp.float32)


SMALL = pltpu.CompilerParams(vmem_limit_bytes=16 * 1024 * 1024)


def call(kernel, ins, outs, scratch, name, aliases=None):
    return pl.pallas_call(
        kernel,
        out_shape=outs,
        in_specs=[VMEM] * len(ins),
        out_specs=[VMEM] * len(outs),
        scratch_shapes=scratch,
        input_output_aliases=aliases or {},
        compiler_params=SMALL,
        name=name,
    )(*ins)


def in_hbm(a):
    return pltpu.with_memory_space_constraint(a, pltpu.HBM)


def to_peers(pieces, axis):
    count = lax.axis_size(axis)
    got = {0: pieces[0]}
    for k in reversed(range(1, count)):
        got[k] = lax.ppermute(pieces[k], axis, [(i, i ^ k) for i in range(count)])
    return [got[k] for k in range(count)]


def line_ghosts(cells, dim, width):
    count = lax.axis_size("gx")
    size = cells.shape[dim]
    head = lax.slice_in_dim(cells, 0, width, axis=dim)
    tail = lax.slice_in_dim(cells, size - width, size, axis=dim)
    if count == 2:
        at_first = lax.axis_index("gx") == 0
        other = lax.ppermute(jnp.where(at_first, tail, head), "gx", [(0, 1), (1, 0)])
        zero = jnp.zeros_like(other)
        return jnp.where(at_first, zero, other), jnp.where(at_first, other, zero)
    ups = [(i, i + 1) for i in range(count - 1)]
    downs = [(i + 1, i) for i in range(count - 1)]
    return lax.ppermute(tail, "gx", ups), lax.ppermute(head, "gx", downs)


def block_tail(blocks, width):
    groups, size = lax.axis_size("gz"), blocks.shape[0]
    start = jnp.where(lax.axis_index("gz") < groups // 2, size - width, 0)
    return lax.dynamic_slice_in_dim(blocks, start, width, 0)


def block_ghosts(tail, own):
    groups, count = lax.axis_size("gz"), lax.axis_size("gx")
    reach = -(-tail.shape[0] // own)
    assert 2 * reach <= groups
    shift = reach if 4 * reach <= groups else 0
    pairs = []
    for g in range(reach):
        for a in range(count - 1):
            pairs.append(((g + shift) * count + a, g * count + a + 1))
            pairs.append(((groups - 1 - g - shift) * count + a + 1, (groups - 1 - g) * count + a))
    return lax.ppermute(tail, ("gz", "gx"), pairs)


def window_ghosts(windows, ready, own, ghost):
    groups, count = lax.axis_size("gz"), lax.axis_size("gx")
    nz_local = windows[0].shape[1]
    (lines,) = call(
        functools.partial(ghost_pack_kernel, "gz", own, ghost),
        [*windows, ready],
        [f32(groups, 2, nz_local, ghost, LANES)],
        [],
        "ghost_pack",
    )
    end = (groups - 1) * count
    pairs = [(end + a, a + 1) for a in range(count - 1)]
    pairs += [(a + 1, end + a) for a in range(count - 1)]
    return lax.ppermute(lines, ("gz", "gx"), pairs)


def refresh_ghosts(planes, ghost):
    split = planes.reshape(planes.shape[0], HALF, 2, HALF)
    groups, count = lax.axis_size("gz"), lax.axis_size("gx")
    places = [g * count + x for x in range(count) for g in range(groups)]
    ups = list(zip(places[:-1], places[1:]))
    downs = list(zip(places[1:], places[:-1]))
    before = lax.ppermute(split[..., HALF - 2 * ghost : HALF - ghost], ("gz", "gx"), ups)
    after = lax.ppermute(split[..., ghost : 2 * ghost], ("gz", "gx"), downs)
    whole = jnp.concatenate([before, split[..., ghost : HALF - ghost], after], axis=-1)
    return whole.reshape(planes.shape)


def body(initial_field, source_term, block_inverse):
    groups, peers = lax.axis_size("gz"), lax.axis_size("gy")
    nz_local, lines, _ = initial_field.shape
    nz = nz_local * groups
    own = lines // groups
    ghost = (HALF - own) // 2
    assert block_inverse.shape[1:] == (LANES, LANES) and lines % groups == 0
    assert nz % STEPS == 0 and nz <= ghost and peers <= 4
    here = lax.axis_index("gz")

    late = own == 2 * ghost
    rows = block_inverse.reshape(lines * LANES, LANES)
    if late:
        chunks = HALF // ghost
        tail = pl.pallas_call(
            functools.partial(tail_kernel, "gz", groups),
            out_shape=f32(ghost, LANES, LANES),
            in_specs=[HBM],
            out_specs=HBM,
            scratch_shapes=[pltpu.SemaphoreType.DMA((4,))],
            compiler_params=PARAMS,
            name="tail",
        )(in_hbm(block_inverse))
        windows = pl.pallas_call(
            functools.partial(pack_kernel, "gz", own, ghost),
            out_shape=[f32(2, nz_local, HALF, LANES)] * groups,
            in_specs=[HBM] * 2,
            out_specs=[VMEM] * groups,
            scratch_shapes=[pltpu.SemaphoreType.DMA((2 * groups * chunks,))],
            compiler_params=PARAMS,
            name="pack",
        )(in_hbm(initial_field), in_hbm(source_term))
    else:
        tail = block_tail(block_inverse, ghost)
        fields = jnp.stack([initial_field, source_term])
        before, after = line_ghosts(fields, 2, ghost)
        wide = jnp.concatenate([before, fields, after], axis=2)
        windows = [
            lax.dynamic_slice_in_dim(wide, jnp.bitwise_xor(here, k) * own, HALF, 2)
            for k in range(groups)
        ]
    beyond = block_ghosts(tail, own).reshape(ghost * LANES, LANES)
    turned = LANES * HALF * LANES * 4
    blocks, ready = pl.pallas_call(
        functools.partial(layout_kernel, own, ghost, "gz"),
        out_shape=[f32(LANES * HALF, LANES), f32(8, LANES)],
        in_specs=[HBM] * (1 if late else 2),
        out_specs=[VMEM, VMEM],
        scratch_shapes=[
            pltpu.VMEM((HALF * LANES, LANES), jnp.float32),
            pltpu.SemaphoreType.DMA((HALF // math.gcd(own, ghost),)),
        ],
        compiler_params=PARAMS,
        cost_estimate=pl.CostEstimate(flops=0, bytes_accessed=4 * turned, transcendentals=0),
        name="layout",
    )(*[in_hbm(a) for a in ([rows] if late else [rows, beyond])])
    fields_here = to_peers(windows, "gz")
    ghosts_here = []
    if late:
        ghosts_here = [window_ghosts(fields_here, ready, own, ghost)]
        blocks = pl.pallas_call(
            functools.partial(patch_kernel, "gz", groups),
            out_shape=f32(LANES * HALF, LANES),
            in_specs=[VMEM, VMEM],
            out_specs=VMEM,
            input_output_aliases={0: 0},
            compiler_params=PARAMS,
            name="patch",
        )(blocks, beyond)


    plane = pltpu.VMEM((HALF, LANES), jnp.float32)
    answers, effects = call(
        responses_kernel,
        [blocks],
        [f32(PACK_ROWS, LANES), f32(PLANES, HALF, LANES)],
        [plane, pltpu.VMEM((PLANES, HALF, LANES), jnp.float32)],
        "responses",
    )
    first_rows = PACK_ROWS + 8 * (-(-nz // 8))
    rhs, loc, *packs = call(
        functools.partial(first_kernel, "gz", groups, late),
        [*fields_here, *ghosts_here, blocks, answers],
        [f32(nz, HALF, LANES), f32(2, HALF, LANES)]
        + [f32(first_rows + 8 * k, LANES) for k in range(peers - 1)],
        [pltpu.VMEM((nz + 2, HALF, LANES), jnp.float32), pltpu.VMEM((nz, HALF, LANES), jnp.float32)]
        + [plane],
        "first_chain",
    )
    schedule = [list(range(a, a + STEPS)) for a in range(0, 2 * nz, STEPS)]
    coef = add = state = None
    for n, steps in enumerate(schedule):
        first = n == 0
        final = n + 1 == len(schedule)
        renew = steps[-1] == nz - 1 and 2 * nz > ghost
        later = None if final or renew else schedule[n + 1]
        packs = to_peers([packs[0], *packs], "gy")
        ins = [*packs, blocks, effects, rhs, loc] + ([] if first else [coef, add, state])
        planes = f32(nz, HALF, LANES)
        outs = [f32(nz, own, LANES)] if final else []
        outs += [planes, planes, f32(HALF, LANES)]
        if later:
            outs += [f32(2, HALF, LANES)] + [f32(8 * k, LANES) for k in range(1, peers)]
        outs += [f32(8, PACK_ROWS, LANES)] if first else []
        at_rhs = 1 if final else 0
        aliases = {peers + 2: at_rhs}
        if not first:
            aliases[peers + 5] = at_rhs + 1
        results = call(
            functools.partial(next_kernel, steps, later, first, peers, "gy", ghost),
            ins,
            outs,
            [
                pltpu.VMEM((8, first_rows if first else 8, LANES), jnp.float32),
                pltpu.VMEM((STEPS + nz, 8, LANES), jnp.float32),
                pltpu.VMEM((PLANES + 2, 8, LANES), jnp.float32),
                plane,
            ],
            "next_chain",
            aliases,
        )
        if final:
            change = results[0]
            break
        rhs, add, state = results[:3]
        if later:
            loc, *packs = results[3 : 3 + peers]
        if first:
            coef = results[-1]
        if renew:
            renewed = refresh_ghosts(jnp.concatenate([rhs, add, state[None]]), ghost)
            rhs, add, state = renewed[:nz], renewed[nz : 2 * nz], renewed[2 * nz]
            loc, *packs = call(
                functools.partial(local_kernel, schedule[n + 1]),
                [blocks, rhs, add, state],
                [f32(2, HALF, LANES)] + [f32(8 * k, LANES) for k in range(1, peers)],
                [plane],
                "local_chain",
            )

    sends = [
        lax.dynamic_slice_in_dim(change, jnp.bitwise_xor(here, k) * nz_local, nz_local, 0)
        for k in range(groups)
    ]
    parts = to_peers(sends, "gz")
    return call(
        functools.partial(finish_kernel, "gz"),
        [initial_field, *parts],
        [f32(*initial_field.shape)],
        [],
        "finish",
    )[0]


def solution(mesh):
    placed = (P("gz", "gx", "gy"), P("gz", "gx", "gy"), P("gx", "gy", None))
    return jax.shard_map(
        body, mesh=mesh, in_specs=placed, out_specs=P("gz", "gx", "gy"), check_vma=False
    )
```

```python
import functools
import math
import jax
import jax.numpy as jnp
from jax import lax
from jax.experimental import pallas as pl
from jax.experimental.pallas import tpu as pltpu
from jax.sharding import PartitionSpec as P

LANES = 128
HALF = 64
STEPS = 4
SPREAD = [(k, side, delta) for k in range(1, STEPS) for side in range(2) for delta in range(1 - k, k)]
PLANES = sum(k <= 2 for k, _, _ in SPREAD)
PACK_ROWS = 8 * (-(-(STEPS + len(SPREAD)) // 8))
VMEM = pl.BlockSpec(memory_space=pltpu.VMEM)
HBM = pl.BlockSpec(memory_space=pltpu.HBM)
PARAMS = pltpu.CompilerParams(vmem_limit_bytes=16 * 1024 * 1024)


def window_of(device):
    if isinstance(device, int):
        return device ^ 1 if device < 2 else device
    return jnp.where(device < 2, jnp.bitwise_xor(device, 1), device)


def low_lanes(rows):
    return lax.broadcasted_iota(jnp.int32, (rows, LANES), 1) < HALF


def swap_halves(a):
    return pltpu.roll(a, HALF, 1)


def from_line(a, delta):
    return a if delta == 0 else pltpu.roll(a, (-delta) % LANES, 1)


def sum_x(a):
    return a + pltpu.roll(a, 1, 1) + pltpu.roll(a, LANES - 1, 1)


def sum_y(a, halo=None):
    low = low_lanes(1)
    first = swap_halves(a[:8])[0:1]
    last = swap_halves(a[HALF - 8 :])[7:8]
    halo = jnp.zeros((1, LANES), jnp.float32) if halo is None else halo
    above = jnp.where(low, halo, last)
    below = jnp.where(low, first, halo)
    row = lax.broadcasted_iota(jnp.int32, a.shape, 0)
    up = jnp.where(row == 0, above, pltpu.roll(a, 1, 0))
    down = jnp.where(row == HALF - 1, below, pltpu.roll(a, HALF - 1, 0))
    return a + up + down


def spread(a):
    low = low_lanes(a.shape[0])
    swapped = swap_halves(a)
    return jnp.where(low, a, swapped), jnp.where(low, swapped, a)


def edges(a):
    return jnp.where(low_lanes(1), a[0:1], a[HALF - 1 : HALF])


def block_column(b_ref, j):
    return b_ref[pl.ds(j, HALF, stride=LANES), :]


def fold_rows(parts):
    row = lax.broadcasted_iota(jnp.int32, (8, LANES), 0)
    for bit in (1, 2, 4):
        first = (row & bit) == 0
        parts = [
            jnp.where(first, a, b) + pltpu.roll(jnp.where(first, b, a), 8 - bit, 0)
            for a, b in zip(parts[::2], parts[1::2])
        ]
    return parts[0]


def apply_blocks(b_ref, rhs, out_ref, arrival=None):
    tiles = [half[8 * t : 8 * t + 8] for half in spread(rhs) for t in range(HALF // 8)]

    def rows(outer, carry):
        if arrival is not None:
            arrival(outer)
        parts = []
        for u in range(8):
            at = (outer * 8 + u) * LANES
            terms = [b_ref[pl.ds(at + 8 * t, 8), :] * tiles[t] for t in range(2)]
            for t in range(2, len(tiles)):
                terms[t % 2] = terms[t % 2] + b_ref[pl.ds(at + 8 * t, 8), :] * tiles[t]
            parts.append(terms[0] + terms[1])
        out_ref[pl.ds(outer * 8, 8), :] = fold_rows(parts)
        return carry

    lax.fori_loop(0, HALF // 8, rows, 0, unroll=True)
    return out_ref[...]


def edge_rows(b_ref):
    return jnp.where(
        low_lanes(LANES), b_ref[0:LANES, :], b_ref[(HALF - 1) * LANES : HALF * LANES, :]
    )


def apply_edges(rows, rhs):
    top, bottom = spread(rhs)
    return jnp.sum(rows[:HALF] * top + rows[HALF:] * bottom, axis=0, keepdims=True)


def layout_kernel(own, ghost, axis, b_ref, *refs):
    *ghost_refs, out_ref, ready_ref, window, sems = refs
    ready_ref[...] = jnp.zeros(ready_ref.shape, jnp.float32)
    ghost_ref = ghost_refs[0] if ghost_refs else b_ref
    count = b_ref.shape[0] // LANES
    position = window_of(lax.axis_index(axis))
    chunk = math.gcd(own, ghost)
    size = chunk * LANES
    copies = []
    for c in range(HALF // chunk):
        start = position * own - ghost + c * chunk
        inside = jnp.logical_and(start >= 0, start < count)
        target = window.at[pl.ds(c * size, size)]
        here = jnp.clip(start, 0, count - chunk)
        beyond = jnp.clip(jnp.where(start < 0, start + ghost, start - count), 0, ghost - chunk)

        @pl.when(inside)
        def _(at=pl.multiple_of(here * LANES, LANES), target=target, c=c):
            pltpu.make_async_copy(b_ref.at[pl.ds(at, size)], target, sems.at[c]).start()

        @pl.when(jnp.logical_not(inside))
        def _(at=pl.multiple_of(beyond * LANES, LANES), target=target, c=c):
            pltpu.make_async_copy(ghost_ref.at[pl.ds(at, size)], target, sems.at[c]).start()

        copies.append(pltpu.make_async_copy(b_ref.at[pl.ds(0, size)], target, sems.at[c]))
    for copy in copies:
        copy.wait()

    def one(outer, carry):
        for u in range(8):
            i = outer * 8 + u
            top = window[pl.ds(i, HALF, stride=LANES), :]
            bottom = window[pl.ds(i + HALF, HALF, stride=LANES), :]
            at = pl.multiple_of(i * LANES, LANES)
            out_ref[pl.ds(at, LANES), :] = jnp.concatenate([top, bottom], axis=0).T
        return carry

    lax.fori_loop(0, HALF // 8, one, 0)


def tail_kernel(axis, groups, b_ref, tail_ref, sems):
    ghost = tail_ref.shape[0]
    start = jnp.where(lax.axis_index(axis) < groups // 2, b_ref.shape[0] - ghost, 0)
    part = ghost // 4
    copies = [
        pltpu.make_async_copy(
            b_ref.at[pl.ds(start + n * part, part)], tail_ref.at[pl.ds(n * part, part)], sems.at[n]
        )
        for n in range(4)
    ]
    for copy in copies:
        copy.start()
    for copy in copies:
        copy.wait()


def pack_kernel(axis, own, ghost, v_ref, s_ref, *refs):
    *window_refs, sems = refs
    position = lax.axis_index(axis)
    last = v_ref.shape[1] - ghost
    copies = []
    for k, window_ref in enumerate(window_refs):
        peer = window_of(jnp.bitwise_xor(position, k))
        for c in range(HALF // ghost):
            at = pl.multiple_of(jnp.clip(peer * own - ghost + c * ghost, 0, last), ghost)
            for kind, ref in enumerate((v_ref, s_ref)):
                copies.append(
                    pltpu.make_async_copy(
                        ref.at[:, pl.ds(at, ghost), :],
                        window_ref.at[kind, :, pl.ds(c * ghost, ghost), :],
                        sems.at[len(copies)],
                    )
                )
    for copy in copies:
        copy.start()
    for copy in copies:
        copy.wait()


def patch_kernel(axis, groups, b_in, beyond, out_ref):
    ghost = beyond.shape[0] // LANES
    per_turn = HALF // ghost
    unroll = 4
    position = window_of(lax.axis_index(axis))
    for place, at in ((0, 0), (groups - 1, HALF - ghost)):

        @pl.when(position == place)
        def _(at=at):
            lane = lax.broadcasted_iota(jnp.int32, (LANES, LANES), 1) % HALF
            mine = jnp.logical_and(lane >= at, lane < at + ghost)

            def one(outer, carry):
                turns = []
                for v in range(unroll):
                    first = (outer * unroll + v) * per_turn
                    rows = [
                        beyond[pl.ds(half * HALF + first + u, ghost, stride=LANES), :]
                        for half in range(2)
                        for u in range(per_turn)
                    ]
                    turns.append(jnp.concatenate(rows, axis=0).T)
                for v in range(unroll):
                    first = (outer * unroll + v) * per_turn
                    for u in range(per_turn):
                        moved = from_line(turns[v], (u * ghost - at) % LANES)
                        here = pl.ds(pl.multiple_of((first + u) * LANES, LANES), LANES)
                        out_ref[here, :] = jnp.where(mine, moved, b_in[here, :])
                return carry

            lax.fori_loop(0, HALF // per_turn // unroll, one, 0)


def responses_kernel(b_ref, pack_ref, plane_ref, r_ref, many_ref):
    pack_ref[...] = jnp.zeros(pack_ref.shape, jnp.float32)
    firsts = [block_column(b_ref, 0), block_column(b_ref, LANES - 1)]
    for side, first in enumerate(firsts):
        many_ref[side] = first
        shifted = sum_y(first)
        for n, (k, at_side, delta) in enumerate(SPREAD):
            if k == 2 and at_side == side:
                many_ref[n] = from_line(shifted, delta)

    def product(n, carry):
        many_ref[n] = apply_blocks(b_ref, many_ref[n], r_ref)
        return carry

    lax.fori_loop(2, PLANES, product, 0, unroll=True)
    second = {SPREAD[n][1:]: many_ref[n] for n in range(2, PLANES)}
    rows = edge_rows(b_ref)
    for n, (k, side, delta) in enumerate(SPREAD):
        if k <= 2:
            row = edges(many_ref[n])
        else:
            parts = [
                from_line(second[side, delta - m], m) for m in (-1, 0, 1) if abs(delta - m) <= 1
            ]
            row = apply_edges(rows, sum_y(sum(parts[1:], parts[0])))
        pack_ref[pl.ds(STEPS + n, 1), :] = row
    plane_ref[...] = many_ref[...]


def planes_of(steps, nz):
    return (steps[0], 1) if steps[0] < nz else (2 * nz - 1 - steps[0], -1)


def local_chain(steps, b_ref, rhs_ref, add_ref, state, r_ref, pack_ref, loc_ref):
    first, move = planes_of(steps, rhs_ref.shape[0])
    if state is None:
        state = jnp.zeros((HALF, LANES), jnp.float32)
    else:
        pack_ref[0:1, :] = edges(state)
    ahead = len(steps) - 2

    def transition(n, state):
        z = first + move * n
        state = apply_blocks(b_ref, rhs_ref[z] + sum_y(sum_x(state)), r_ref)
        if move < 0:
            state = state + add_ref[z]
        loc_ref[n] = state
        pack_ref[pl.ds(n + 1, 1), :] = edges(state)
        return state

    state = lax.fori_loop(0, ahead, transition, state, unroll=True)
    z = first + move * ahead
    row = apply_edges(edge_rows(b_ref), rhs_ref[z] + sum_y(sum_x(state)))
    pack_ref[ahead + 1 : ahead + 2, :] = row + edges(add_ref[z]) if move < 0 else row


def copy_pack(pack_refs):
    first = pack_refs[0][...]
    for ref in pack_refs[1:]:
        ref[: first.shape[0], :] = first
        ref[first.shape[0] :, :] = jnp.zeros((ref.shape[0] - first.shape[0], LANES), jnp.float32)


def gather_planes(axis, groups, field_refs, ghost_ref, v_ref, s_ref):
    position = lax.axis_index(axis)
    window = window_of(position)
    senders = window_of(0) ^ window_of(groups - 1)
    low = low_lanes(HALF)
    nz_local = field_refs[0].shape[1]
    for k, ref in enumerate(field_refs):
        base = jnp.bitwise_xor(position, k) * nz_local
        for p in range(nz_local):
            for kind, target in ((0, v_ref), (1, s_ref)):
                plane = ref[kind, p]
                if ghost_ref is not None:
                    beyond = ghost_ref[senders ^ k, kind, p]
                    ghost = beyond.shape[0]
                    first = jnp.where(window == 0, beyond, plane[:ghost])
                    last = jnp.where(window == groups - 1, beyond, plane[HALF - ghost :])
                    plane = jnp.concatenate([first, plane[ghost : HALF - ghost], last], axis=0)
                turned = jnp.concatenate([plane, plane], axis=0).T
                target[base + p + 1 - kind] = jnp.where(low, turned[:HALF], turned[HALF:])


def first_kernel(axis, fields, late, *refs):
    field_refs = refs[:fields]
    ghost_ref = refs[fields] if late else None
    refs = refs[1:] if late else refs
    b_ref, answers_ref, rhs_ref, loc_ref, *pack_refs, v_ref, s_ref, r_ref = refs[fields:]
    pack_ref = pack_refs[0]
    nz = rhs_ref.shape[0]
    pack_ref[...] = jnp.zeros(pack_ref.shape, jnp.float32)
    pack_ref[:PACK_ROWS, :] = answers_ref[...]
    v_ref[0] = jnp.zeros((HALF, LANES), jnp.float32)
    v_ref[nz + 1] = jnp.zeros((HALF, LANES), jnp.float32)
    gather_planes(axis, fields, field_refs, ghost_ref, v_ref, s_ref)
    for z in range(nz):
        around = v_ref[z] + v_ref[z + 1] + v_ref[z + 2]
        rhs_ref[z] = s_ref[z] - 27.0 * v_ref[z + 1] + sum_y(sum_x(around))
        pack_ref[PACK_ROWS + z : PACK_ROWS + z + 1, :] = edges(around)
    local_chain(list(range(STEPS)), b_ref, rhs_ref, None, None, r_ref, pack_ref, loc_ref)
    copy_pack(pack_refs)


def beside(ends, swapped):
    low = low_lanes(8)
    left = pltpu.roll(jnp.where(low, swapped, ends), 1, 0)
    right = pltpu.roll(jnp.where(low, ends, swapped), 7, 0)
    return left, right


def complete_edges(first, gather, coef_ref, halo_ref, inject_ref):
    low = low_lanes(8)
    known = [gather[:, t, :] for t in range(STEPS)]
    totals = [(row, swap_halves(row)) for row in known]
    for t in range(STEPS):
        halo = None if first and t == 0 else beside(*totals[t])
        if halo is None:
            halo_ref[t] = jnp.zeros((8, LANES), jnp.float32)
        else:
            halo_ref[t] = sum_x(jnp.where(low, *halo))
        if first:
            row = gather[:, PACK_ROWS + t, :]
            start = beside(row, swap_halves(row))
            halo = start if halo is None else [x + y for x, y in zip(halo, start)]
        reach = STEPS - 1 - t
        width = max(reach - 1, 1 if t == 0 else 0)
        if reach < 1:
            break
        summed = []
        for cells in halo:
            moved = {m: from_line(cells, m) for m in range(-width - 1, width + 2)}
            summed.append(
                {m: moved[m - 1] + moved[m] + moved[m + 1] for m in range(-width, width + 1)}
            )
        for n, (k, side, delta) in enumerate(SPREAD):
            if k <= reach:
                coef = coef_ref[:, STEPS + n, :]
                ends, swapped = totals[t + k]
                totals[t + k] = (
                    ends + coef * summed[side][delta],
                    swapped + swap_halves(coef) * summed[side][delta],
                )
        if t < 2:
            for n, (k, side, delta) in enumerate(SPREAD[: PLANES if t == 0 else 2]):
                inject_ref[t * PLANES + n] = summed[side][delta]


def ghost_pack_kernel(axis, own, ghost, *refs):
    *window_refs, ready_ref, out_ref = refs
    at = jnp.where(window_of(lax.axis_index(axis)) == 0, ghost, own)
    for k, ref in enumerate(window_refs):
        out_ref[k] = ref[:, :, pl.ds(pl.multiple_of(at, 8), ghost), :]


def next_kernel(steps, later, first, peers, axis, ghost, *refs):
    refs = list(refs)

    def take(count):
        taken = refs[:count]
        del refs[:count]
        return taken

    packs = take(peers)
    b_ref, plane_ref, rhs_in, loc_in = take(4)
    coef_ref, add_in, state_in = (None, None, None) if first else take(3)
    last = steps is not None and steps[-1] == 2 * rhs_in.shape[0] - 1
    if last:
        (out_ref,) = take(1)
        rhs_ref, state_ref, add_ref = rhs_in, None, refs.pop()
        add_ref[...] = add_in[...]
    else:
        rhs_ref, add_ref, state_ref = take(3)
    loc_ref, *pack_refs = take(peers) if later else (None,)
    coef_out = take(1)[0] if first else None
    gather, halo_ref, inject_ref, r_ref, *own_copy = refs
    nz = rhs_in.shape[0]
    position = lax.axis_index(axis)
    arrival = None
    if last:
        b_hbm, (b_ref, sems) = b_ref, own_copy
        size = 8 * LANES
        copies = [
            pltpu.make_async_copy(
                b_hbm.at[pl.ds(n * size, size)], b_ref.at[pl.ds(n * size, size)], sems.at[n]
            )
            for n in range(HALF // 8)
        ]
        for copy in copies:
            copy.start()

        def arrival(n):
            at = pl.ds(n * size, size)
            pltpu.make_async_copy(b_hbm.at[at], b_ref.at[at], sems.at[n]).wait()

    gather[...] = jnp.zeros(gather.shape, jnp.float32)
    for k in range(peers):
        gather[jnp.bitwise_xor(position, k)] = packs[k][: gather.shape[1], :]
    if first:
        coef_out[...] = gather[:, :PACK_ROWS, :]
    complete_edges(first, gather, gather if first else coef_ref, halo_ref, inject_ref)
    own = pl.ds(position, 1)
    low = low_lanes(HALF)
    row_index = lax.broadcasted_iota(jnp.int32, (HALF, LANES), 0)
    if first:
        for z in range(nz):
            row = gather[:, PACK_ROWS + z, :]
            left, right = beside(row, swap_halves(row))
            halo_ref[STEPS + z] = sum_x(jnp.where(low_lanes(8), left, right))
            halo = halo_ref[STEPS + z, own, :]
            at_edge = jnp.logical_or(
                jnp.logical_and(row_index == 0, low),
                jnp.logical_and(row_index == HALF - 1, jnp.logical_not(low)),
            )
            rhs_ref[z] = rhs_ref[z] + jnp.where(at_edge, halo, 0.0)

    first_plane, move = planes_of(steps, nz)

    def keep(z, state):
        add_ref[z] = 2.0 * state if move > 0 else state

    if not first:
        state = state_in[...]
        if move > 0:
            around = sum_y(sum_x(state), halo_ref[0, own, :])
            rhs_ref[first_plane - 1] = around - 27.0 * state
    state = loc_in[0]
    for n in range(2):
        state = state + plane_ref[n] * inject_ref[n, own, :]
    keep(first_plane, state)
    if move > 0:
        rhs_ref[first_plane] = sum_y(sum_x(state), halo_ref[1, own, :]) - 27.0 * state
    state = loc_in[1]
    for n in range(PLANES):
        state = state + plane_ref[n] * inject_ref[n if n >= 2 else PLANES + n, own, :]
    keep(first_plane + move, state)

    for t in range(2, STEPS):
        z = first_plane + move * t
        around = sum_y(sum_x(state), halo_ref[t, own, :])
        if move > 0:
            rhs_ref[z - 1] = around - 27.0 * state
        state = apply_blocks(b_ref, rhs_ref[z] + around, r_ref, arrival if t == 2 else None)
        if move < 0:
            state = state + add_ref[z]
        keep(z, state)
    if steps[-1] == nz - 1:
        rhs_ref[nz - 1] = -27.0 * state
    if not last:
        state_ref[...] = state
    if later:
        pack_ref = pack_refs[0]
        pack_ref[...] = jnp.zeros(pack_ref.shape, jnp.float32)
        local_chain(later, b_ref, rhs_ref, add_ref, state, r_ref, pack_ref, loc_ref)
        copy_pack(pack_refs)
    if last:
        own_lines = HALF - 2 * ghost
        for z in range(nz):
            plane = add_ref[z]
            turned = jnp.concatenate([plane, swap_halves(plane)], axis=0).T
            out_ref[z] = turned[ghost : ghost + own_lines]


def local_kernel(steps, b_ref, rhs_ref, add_ref, state_ref, loc_ref, *refs):
    *pack_refs, r_ref = refs
    pack_refs[0][...] = jnp.zeros(pack_refs[0].shape, jnp.float32)
    local_chain(steps, b_ref, rhs_ref, add_ref, state_ref[...], r_ref, pack_refs[0], loc_ref)
    copy_pack(pack_refs)


def finish_kernel(axis, v_ref, *refs):
    parts, out_ref = refs[:-1], refs[-1]
    position = lax.axis_index(axis)
    lines = parts[0].shape[1]
    for k, part in enumerate(parts):
        at = pl.ds(pl.multiple_of(window_of(jnp.bitwise_xor(position, k)) * lines, lines), lines)
        out_ref[:, at, :] = v_ref[:, at, :] + part[...]


def f32(*shape):
    return jax.ShapeDtypeStruct(shape, jnp.float32)


SMALL = pltpu.CompilerParams(vmem_limit_bytes=16 * 1024 * 1024)


def call(kernel, ins, outs, scratch, name, aliases=None, hbm=()):
    return pl.pallas_call(
        kernel,
        out_shape=outs,
        in_specs=[HBM if n in hbm else VMEM for n in range(len(ins))],
        out_specs=[VMEM] * len(outs),
        scratch_shapes=scratch,
        input_output_aliases=aliases or {},
        compiler_params=SMALL,
        name=name,
    )(*[in_hbm(x) if n in hbm else x for n, x in enumerate(ins)])


def in_hbm(a):
    return pltpu.with_memory_space_constraint(a, pltpu.HBM)


def to_peers(pieces, axis):
    count = lax.axis_size(axis)
    got = {0: pieces[0]}
    for k in reversed(range(1, count)):
        got[k] = lax.ppermute(pieces[k], axis, [(i, i ^ k) for i in range(count)])
    return [got[k] for k in range(count)]


def line_ghosts(cells, dim, width):
    count = lax.axis_size("gx")
    size = cells.shape[dim]
    head = lax.slice_in_dim(cells, 0, width, axis=dim)
    tail = lax.slice_in_dim(cells, size - width, size, axis=dim)
    if count == 2:
        at_first = lax.axis_index("gx") == 0
        other = lax.ppermute(jnp.where(at_first, tail, head), "gx", [(0, 1), (1, 0)])
        zero = jnp.zeros_like(other)
        return jnp.where(at_first, zero, other), jnp.where(at_first, other, zero)
    ups = [(i, i + 1) for i in range(count - 1)]
    downs = [(i + 1, i) for i in range(count - 1)]
    return lax.ppermute(tail, "gx", ups), lax.ppermute(head, "gx", downs)


def block_tail(blocks, width):
    groups, size = lax.axis_size("gz"), blocks.shape[0]
    start = jnp.where(lax.axis_index("gz") < groups // 2, size - width, 0)
    return lax.dynamic_slice_in_dim(blocks, start, width, 0)


def block_ghosts(tail, own):
    groups, count = lax.axis_size("gz"), lax.axis_size("gx")
    reach = -(-tail.shape[0] // own)
    assert 2 * reach <= groups
    pairs = []
    for strip in range(reach):
        low, high = window_of(strip), window_of(groups - 1 - strip)
        for a in range(count - 1):
            pairs.append((low * count + a, low * count + a + 1))
            pairs.append((high * count + a + 1, high * count + a))
    return lax.ppermute(tail, ("gz", "gx"), pairs)


def window_ghosts(windows, ready, own, ghost):
    groups, count = lax.axis_size("gz"), lax.axis_size("gx")
    nz_local = windows[0].shape[1]
    (lines,) = call(
        functools.partial(ghost_pack_kernel, "gz", own, ghost),
        [*windows, ready],
        [f32(groups, 2, nz_local, ghost, LANES)],
        [],
        "ghost_pack",
    )
    low, high = window_of(0) * count, window_of(groups - 1) * count
    pairs = [(high + a, low + a + 1) for a in range(count - 1)]
    pairs += [(low + a + 1, high + a) for a in range(count - 1)]
    return lax.ppermute(lines, ("gz", "gx"), pairs)


def refresh_ghosts(planes, ghost):
    split = planes.reshape(planes.shape[0], HALF, 2, HALF)
    groups, count = lax.axis_size("gz"), lax.axis_size("gx")
    places = [window_of(w) * count + x for x in range(count) for w in range(groups)]
    ups = list(zip(places[:-1], places[1:]))
    downs = list(zip(places[1:], places[:-1]))
    before = lax.ppermute(split[..., HALF - 2 * ghost : HALF - ghost], ("gz", "gx"), ups)
    after = lax.ppermute(split[..., ghost : 2 * ghost], ("gz", "gx"), downs)
    whole = jnp.concatenate([before, split[..., ghost : HALF - ghost], after], axis=-1)
    return whole.reshape(planes.shape)


def body(initial_field, source_term, block_inverse):
    groups, peers = lax.axis_size("gz"), lax.axis_size("gy")
    nz_local, lines, _ = initial_field.shape
    nz = nz_local * groups
    own = lines // groups
    ghost = (HALF - own) // 2
    assert block_inverse.shape[1:] == (LANES, LANES) and lines % groups == 0
    assert nz % STEPS == 0 and nz <= ghost and peers <= 4
    here = lax.axis_index("gz")

    late = own == 2 * ghost
    rows = block_inverse.reshape(lines * LANES, LANES)
    if late:
        chunks = HALF // ghost
        tail = pl.pallas_call(
            functools.partial(tail_kernel, "gz", groups),
            out_shape=f32(ghost, LANES, LANES),
            in_specs=[HBM],
            out_specs=VMEM,
            scratch_shapes=[pltpu.SemaphoreType.DMA((4,))],
            compiler_params=PARAMS,
            name="tail",
        )(in_hbm(block_inverse))
        windows = pl.pallas_call(
            functools.partial(pack_kernel, "gz", own, ghost),
            out_shape=[f32(2, nz_local, HALF, LANES)] * groups,
            in_specs=[HBM] * 2,
            out_specs=[VMEM] * groups,
            scratch_shapes=[pltpu.SemaphoreType.DMA((2 * groups * chunks,))],
            compiler_params=PARAMS,
            name="pack",
        )(in_hbm(initial_field), in_hbm(source_term))
    else:
        tail = block_tail(block_inverse, ghost)
        fields = jnp.stack([initial_field, source_term])
        before, after = line_ghosts(fields, 2, ghost)
        wide = jnp.concatenate([before, fields, after], axis=2)
        windows = [
            lax.dynamic_slice_in_dim(wide, window_of(jnp.bitwise_xor(here, k)) * own, HALF, 2)
            for k in range(groups)
        ]
    beyond = block_ghosts(tail, own).reshape(ghost * LANES, LANES)
    turned = LANES * HALF * LANES * 4
    blocks, ready = pl.pallas_call(
        functools.partial(layout_kernel, own, ghost, "gz"),
        out_shape=[f32(LANES * HALF, LANES), f32(8, LANES)],
        in_specs=[HBM] * (1 if late else 2),
        out_specs=[VMEM, VMEM],
        scratch_shapes=[
            pltpu.VMEM((HALF * LANES, LANES), jnp.float32),
            pltpu.SemaphoreType.DMA((HALF // math.gcd(own, ghost),)),
        ],
        compiler_params=PARAMS,
        cost_estimate=pl.CostEstimate(flops=0, bytes_accessed=4 * turned, transcendentals=0),
        name="layout",
    )(*[in_hbm(a) for a in ([rows] if late else [rows, beyond])])
    fields_here = to_peers(windows, "gz")
    ghosts_here = []
    if late:
        ghosts_here = [window_ghosts(fields_here, ready, own, ghost)]
        blocks = pl.pallas_call(
            functools.partial(patch_kernel, "gz", groups),
            out_shape=f32(LANES * HALF, LANES),
            in_specs=[VMEM, VMEM],
            out_specs=VMEM,
            input_output_aliases={0: 0},
            compiler_params=PARAMS,
            name="patch",
        )(blocks, beyond)


    plane = pltpu.VMEM((HALF, LANES), jnp.float32)
    answers, effects = call(
        responses_kernel,
        [blocks],
        [f32(PACK_ROWS, LANES), f32(PLANES, HALF, LANES)],
        [plane, pltpu.VMEM((PLANES, HALF, LANES), jnp.float32)],
        "responses",
    )
    first_rows = PACK_ROWS + 8 * (-(-nz // 8))
    rhs, loc, *packs = call(
        functools.partial(first_kernel, "gz", groups, late),
        [*fields_here, *ghosts_here, blocks, answers],
        [f32(nz, HALF, LANES), f32(2, HALF, LANES)]
        + [f32(first_rows + 8 * k, LANES) for k in range(peers - 1)],
        [pltpu.VMEM((nz + 2, HALF, LANES), jnp.float32), pltpu.VMEM((nz, HALF, LANES), jnp.float32)]
        + [plane],
        "first_chain",
    )
    schedule = [list(range(a, a + STEPS)) for a in range(0, 2 * nz, STEPS)]
    coef = add = state = None
    for n, steps in enumerate(schedule):
        first = n == 0
        final = n + 1 == len(schedule)
        renew = steps[-1] == nz - 1 and 2 * nz > ghost
        later = None if final or renew else schedule[n + 1]
        packs = to_peers([packs[0], *packs], "gy")
        ins = [*packs, blocks, effects, rhs, loc] + ([] if first else [coef, add, state])
        planes = f32(nz, HALF, LANES)
        outs = [f32(nz, own, LANES)] if final else [planes, planes, f32(HALF, LANES)]
        if later:
            outs += [f32(2, HALF, LANES)] + [f32(8 * k, LANES) for k in range(1, peers)]
        outs += [f32(8, PACK_ROWS, LANES)] if first else []
        aliases = {} if final else {peers + 2: 0}
        if not first and not final:
            aliases[peers + 5] = 1
        results = call(
            functools.partial(next_kernel, steps, later, first, peers, "gy", ghost),
            ins,
            outs,
            [
                pltpu.VMEM((8, first_rows if first else 8, LANES), jnp.float32),
                pltpu.VMEM((STEPS + nz, 8, LANES), jnp.float32),
                pltpu.VMEM((PLANES + 2, 8, LANES), jnp.float32),
                plane,
            ]
            + (
                [
                    pltpu.VMEM((LANES * HALF, LANES), jnp.float32),
                    pltpu.SemaphoreType.DMA((HALF // 8,)),
                    pltpu.VMEM((nz, HALF, LANES), jnp.float32),
                ]
                if final
                else []
            ),
            "next_chain",
            aliases,
            (peers,) if final else (),
        )
        if final:
            change = results[0]
            break
        rhs, add, state = results[:3]
        if later:
            loc, *packs = results[3 : 3 + peers]
        if first:
            coef = results[-1]
        if renew:
            renewed = refresh_ghosts(jnp.concatenate([rhs, add, state[None]]), ghost)
            rhs, add, state = renewed[:nz], renewed[nz : 2 * nz], renewed[2 * nz]
            loc, *packs = call(
                functools.partial(local_kernel, schedule[n + 1]),
                [blocks, rhs, add, state],
                [f32(2, HALF, LANES)] + [f32(8 * k, LANES) for k in range(1, peers)],
                [plane],
                "local_chain",
            )

    sends = [
        lax.dynamic_slice_in_dim(change, jnp.bitwise_xor(here, k) * nz_local, nz_local, 0)
        for k in range(groups)
    ]
    parts = to_peers(sends, "gz")
    return call(
        functools.partial(finish_kernel, "gz"),
        [initial_field, *parts],
        [f32(*initial_field.shape)],
        [],
        "finish",
    )[0]


def solution(mesh):
    placed = (P("gz", "gx", "gy"), P("gz", "gx", "gy"), P("gx", "gy", None))
    return jax.shard_map(
        body, mesh=mesh, in_specs=placed, out_specs=P("gz", "gx", "gy"), check_vma=False
    )
```

```python
import functools
import math
import jax
import jax.numpy as jnp
from jax import lax
from jax.experimental import pallas as pl
from jax.experimental.pallas import tpu as pltpu
from jax.sharding import PartitionSpec as P

LANES = 128
HALF = 64
STEPS = 4
SPREAD = [(k, side, delta) for k in range(1, STEPS) for side in range(2) for delta in range(1 - k, k)]
PLANES = sum(k <= 2 for k, _, _ in SPREAD)
PACK_ROWS = 8 * (-(-(STEPS + len(SPREAD)) // 8))
VMEM = pl.BlockSpec(memory_space=pltpu.VMEM)
HBM = pl.BlockSpec(memory_space=pltpu.HBM)
PARAMS = pltpu.CompilerParams(vmem_limit_bytes=16 * 1024 * 1024)


def window_of(device):
    if isinstance(device, int):
        return device ^ 1 if device < 2 else device
    return jnp.where(device < 2, jnp.bitwise_xor(device, 1), device)


def low_lanes(rows):
    return lax.broadcasted_iota(jnp.int32, (rows, LANES), 1) < HALF


def swap_halves(a):
    return pltpu.roll(a, HALF, 1)


def from_line(a, delta):
    return a if delta == 0 else pltpu.roll(a, (-delta) % LANES, 1)


def sum_x(a):
    return a + pltpu.roll(a, 1, 1) + pltpu.roll(a, LANES - 1, 1)


def sum_y(a, halo=None):
    low = low_lanes(1)
    first = swap_halves(a[:8])[0:1]
    last = swap_halves(a[HALF - 8 :])[7:8]
    halo = jnp.zeros((1, LANES), jnp.float32) if halo is None else halo
    above = jnp.where(low, halo, last)
    below = jnp.where(low, first, halo)
    row = lax.broadcasted_iota(jnp.int32, a.shape, 0)
    up = jnp.where(row == 0, above, pltpu.roll(a, 1, 0))
    down = jnp.where(row == HALF - 1, below, pltpu.roll(a, HALF - 1, 0))
    return a + up + down


def spread(a):
    low = low_lanes(a.shape[0])
    swapped = swap_halves(a)
    return jnp.where(low, a, swapped), jnp.where(low, swapped, a)


def edges(a):
    return jnp.where(low_lanes(1), a[0:1], a[HALF - 1 : HALF])


def block_column(b_ref, j):
    return b_ref[pl.ds(j, HALF, stride=LANES), :]


def fold_rows(parts):
    row = lax.broadcasted_iota(jnp.int32, (8, LANES), 0)
    for bit in (1, 2, 4):
        first = (row & bit) == 0
        parts = [
            jnp.where(first, a, b) + pltpu.roll(jnp.where(first, b, a), 8 - bit, 0)
            for a, b in zip(parts[::2], parts[1::2])
        ]
    return parts[0]


def apply_blocks(b_ref, rhs, out_ref, arrival=None):
    tiles = [half[8 * t : 8 * t + 8] for half in spread(rhs) for t in range(HALF // 8)]

    def rows(outer, carry):
        if arrival is not None:
            arrival(outer)
        parts = []
        for u in range(8):
            at = (outer * 8 + u) * LANES
            terms = [b_ref[pl.ds(at + 8 * t, 8), :] * tiles[t] for t in range(2)]
            for t in range(2, len(tiles)):
                terms[t % 2] = terms[t % 2] + b_ref[pl.ds(at + 8 * t, 8), :] * tiles[t]
            parts.append(terms[0] + terms[1])
        out_ref[pl.ds(outer * 8, 8), :] = fold_rows(parts)
        return carry

    lax.fori_loop(0, HALF // 8, rows, 0, unroll=True)
    return out_ref[...]


def edge_rows(b_ref):
    return jnp.where(
        low_lanes(LANES), b_ref[0:LANES, :], b_ref[(HALF - 1) * LANES : HALF * LANES, :]
    )


def apply_edges(rows, rhs):
    top, bottom = spread(rhs)
    return jnp.sum(rows[:HALF] * top + rows[HALF:] * bottom, axis=0, keepdims=True)


def layout_kernel(own, ghost, axis, b_ref, *refs):
    *ghost_refs, out_ref, window, sems = refs
    ghost_ref = ghost_refs[0] if ghost_refs else b_ref
    count = b_ref.shape[0] // LANES
    position = window_of(lax.axis_index(axis))
    chunk = math.gcd(own, ghost)
    size = chunk * LANES
    copies = []
    for c in range(HALF // chunk):
        start = position * own - ghost + c * chunk
        inside = jnp.logical_and(start >= 0, start < count)
        target = window.at[pl.ds(c * size, size)]
        here = jnp.clip(start, 0, count - chunk)
        beyond = jnp.clip(jnp.where(start < 0, start + ghost, start - count), 0, ghost - chunk)

        @pl.when(inside)
        def _(at=pl.multiple_of(here * LANES, LANES), target=target, c=c):
            pltpu.make_async_copy(b_ref.at[pl.ds(at, size)], target, sems.at[c]).start()

        @pl.when(jnp.logical_not(inside))
        def _(at=pl.multiple_of(beyond * LANES, LANES), target=target, c=c):
            pltpu.make_async_copy(ghost_ref.at[pl.ds(at, size)], target, sems.at[c]).start()

        copies.append(pltpu.make_async_copy(b_ref.at[pl.ds(0, size)], target, sems.at[c]))
    for copy in copies:
        copy.wait()

    lax.fori_loop(0, HALF // 8, functools.partial(turn_rows, window, out_ref), 0)


def turn_rows(window, out_ref, outer, carry):
    for u in range(8):
        i = outer * 8 + u
        top = window[pl.ds(i, HALF, stride=LANES), :]
        bottom = window[pl.ds(i + HALF, HALF, stride=LANES), :]
        at = pl.multiple_of(i * LANES, LANES)
        out_ref[pl.ds(at, LANES), :] = jnp.concatenate([top, bottom], axis=0).T
    return carry


def strip_kernel(own, ghost, axis, b_ref, out_ref, window, sems):
    position = window_of(lax.axis_index(axis))
    parts = sems.shape[0]
    size = HALF // parts
    copies = [[] for _ in range(parts)]
    for n in range(parts):
        for half in range(2):
            rows = pl.ds(half * HALF + n * size, size)
            for c in range(HALF // ghost):
                at = jnp.clip(position * own - ghost + c * ghost, 0, b_ref.shape[0] - ghost)
                copies[n].append(
                    pltpu.make_async_copy(
                        b_ref.at[pl.ds(at, ghost), rows, :],
                        window.at[pl.ds(c * ghost, ghost), rows, :],
                        sems.at[n, half, c],
                    )
                )
    for copy in sum(copies, []):
        copy.start()
    flat = window.reshape(HALF * LANES, LANES)
    for n in range(parts):
        for copy in copies[n]:
            copy.wait()
        turn = functools.partial(turn_rows, flat, out_ref)
        lax.fori_loop(n * size // 8, (n + 1) * size // 8, turn, 0)


def tail_kernel(axis, groups, b_ref, tail_ref, sems):
    ghost = tail_ref.shape[0]
    start = jnp.where(lax.axis_index(axis) < groups // 2, b_ref.shape[0] - ghost, 0)
    part = ghost // 4
    copies = [
        pltpu.make_async_copy(
            b_ref.at[pl.ds(start + n * part, part)], tail_ref.at[pl.ds(n * part, part)], sems.at[n]
        )
        for n in range(4)
    ]
    for copy in copies:
        copy.start()
    for copy in copies:
        copy.wait()


def pack_kernel(axis, own, ghost, v_ref, s_ref, *refs):
    *window_refs, sems = refs
    position = lax.axis_index(axis)
    last = v_ref.shape[1] - ghost
    copies = []
    for k, window_ref in enumerate(window_refs):
        peer = window_of(jnp.bitwise_xor(position, k))
        for c in range(HALF // ghost):
            at = pl.multiple_of(jnp.clip(peer * own - ghost + c * ghost, 0, last), ghost)
            for kind, ref in enumerate((v_ref, s_ref)):
                copies.append(
                    pltpu.make_async_copy(
                        ref.at[:, pl.ds(at, ghost), :],
                        window_ref.at[kind, :, pl.ds(c * ghost, ghost), :],
                        sems.at[len(copies)],
                    )
                )
    for copy in copies:
        copy.start()
    for copy in copies:
        copy.wait()


def patch_kernel(axis, groups, b_in, beyond, early_ref, out_ref):
    ghost = beyond.shape[0] // LANES
    per_turn = HALF // ghost
    unroll = 4
    position = window_of(lax.axis_index(axis))
    for place, at in ((0, 0), (groups - 1, HALF - ghost)):

        @pl.when(position == place)
        def _(at=at):
            lane = lax.broadcasted_iota(jnp.int32, (LANES, LANES), 1) % HALF
            mine = jnp.logical_and(lane >= at, lane < at + ghost)

            def one(outer, carry):
                turns = []
                for v in range(unroll):
                    first = (outer * unroll + v) * per_turn
                    rows = [
                        beyond[pl.ds(half * HALF + first + u, ghost, stride=LANES), :]
                        for half in range(2)
                        for u in range(per_turn)
                    ]
                    turns.append(jnp.concatenate(rows, axis=0).T)
                for v in range(unroll):
                    first = (outer * unroll + v) * per_turn
                    for u in range(per_turn):
                        moved = from_line(turns[v], (u * ghost - at) % LANES)
                        here = pl.ds(pl.multiple_of((first + u) * LANES, LANES), LANES)
                        out_ref[here, :] = jnp.where(mine, moved, b_in[here, :])
                return carry

            lax.fori_loop(0, HALF // per_turn // unroll, one, 0)


def responses_kernel(groups, at_end, b_ref, *refs):
    pack_ref, plane_ref, r_ref, many_ref = refs[-4:]
    if at_end is None:
        responses(b_ref, pack_ref, plane_ref, r_ref, many_ref)
        return
    window = window_of(lax.axis_index("gz"))
    ends = jnp.logical_or(window == 0, window == groups - 1)

    @pl.when(ends if at_end else jnp.logical_not(ends))
    def _():
        responses(b_ref, pack_ref, plane_ref, r_ref, many_ref)


def responses(b_ref, pack_ref, plane_ref, r_ref, many_ref):
    pack_ref[...] = jnp.zeros(pack_ref.shape, jnp.float32)
    firsts = [block_column(b_ref, 0), block_column(b_ref, LANES - 1)]
    for side, first in enumerate(firsts):
        many_ref[side] = first
        shifted = sum_y(first)
        for n, (k, at_side, delta) in enumerate(SPREAD):
            if k == 2 and at_side == side:
                many_ref[n] = from_line(shifted, delta)

    def product(n, carry):
        many_ref[n] = apply_blocks(b_ref, many_ref[n], r_ref)
        return carry

    lax.fori_loop(2, PLANES, product, 0, unroll=True)
    second = {SPREAD[n][1:]: many_ref[n] for n in range(2, PLANES)}
    rows = edge_rows(b_ref)
    for n, (k, side, delta) in enumerate(SPREAD):
        if k <= 2:
            row = edges(many_ref[n])
        else:
            parts = [
                from_line(second[side, delta - m], m) for m in (-1, 0, 1) if abs(delta - m) <= 1
            ]
            row = apply_edges(rows, sum_y(sum(parts[1:], parts[0])))
        pack_ref[pl.ds(STEPS + n, 1), :] = row
    plane_ref[...] = many_ref[...]


def planes_of(steps, nz):
    return (steps[0], 1) if steps[0] < nz else (2 * nz - 1 - steps[0], -1)


def local_chain(steps, b_ref, rhs_ref, add_ref, state, r_ref, pack_ref, loc_ref):
    first, move = planes_of(steps, rhs_ref.shape[0])
    if state is None:
        state = jnp.zeros((HALF, LANES), jnp.float32)
    else:
        pack_ref[0:1, :] = edges(state)
    ahead = len(steps) - 2

    def transition(n, state):
        z = first + move * n
        state = apply_blocks(b_ref, rhs_ref[z] + sum_y(sum_x(state)), r_ref)
        if move < 0:
            state = state + add_ref[z]
        loc_ref[n] = state
        pack_ref[pl.ds(n + 1, 1), :] = edges(state)
        return state

    state = lax.fori_loop(0, ahead, transition, state, unroll=True)
    z = first + move * ahead
    row = apply_edges(edge_rows(b_ref), rhs_ref[z] + sum_y(sum_x(state)))
    pack_ref[ahead + 1 : ahead + 2, :] = row + edges(add_ref[z]) if move < 0 else row


def copy_pack(pack_refs):
    first = pack_refs[0][...]
    for ref in pack_refs[1:]:
        ref[: first.shape[0], :] = first
        ref[first.shape[0] :, :] = jnp.zeros((ref.shape[0] - first.shape[0], LANES), jnp.float32)


def gather_planes(axis, groups, field_refs, ghost_ref, v_ref, s_ref):
    position = lax.axis_index(axis)
    window = window_of(position)
    senders = window_of(0) ^ window_of(groups - 1)
    low = low_lanes(HALF)
    nz_local = field_refs[0].shape[1]
    for k, ref in enumerate(field_refs):
        base = jnp.bitwise_xor(position, k) * nz_local
        for p in range(nz_local):
            for kind, target in ((0, v_ref), (1, s_ref)):
                plane = ref[kind, p]
                if ghost_ref is not None:
                    beyond = ghost_ref[senders ^ k, kind, p]
                    ghost = beyond.shape[0]
                    first = jnp.where(window == 0, beyond, plane[:ghost])
                    last = jnp.where(window == groups - 1, beyond, plane[HALF - ghost :])
                    plane = jnp.concatenate([first, plane[ghost : HALF - ghost], last], axis=0)
                turned = jnp.concatenate([plane, plane], axis=0).T
                target[base + p + 1 - kind] = jnp.where(low, turned[:HALF], turned[HALF:])


def first_kernel(axis, fields, late, *refs):
    field_refs = refs[:fields]
    ghost_ref = refs[fields] if late else None
    refs = refs[1:] if late else refs
    b_ref, answers_ref, rhs_ref, loc_ref, *pack_refs, v_ref, s_ref, r_ref = refs[fields:]
    pack_ref = pack_refs[0]
    nz = rhs_ref.shape[0]
    pack_ref[...] = jnp.zeros(pack_ref.shape, jnp.float32)
    pack_ref[:PACK_ROWS, :] = answers_ref[...]
    v_ref[0] = jnp.zeros((HALF, LANES), jnp.float32)
    v_ref[nz + 1] = jnp.zeros((HALF, LANES), jnp.float32)
    gather_planes(axis, fields, field_refs, ghost_ref, v_ref, s_ref)
    for z in range(nz):
        around = v_ref[z] + v_ref[z + 1] + v_ref[z + 2]
        rhs_ref[z] = s_ref[z] - 27.0 * v_ref[z + 1] + sum_y(sum_x(around))
        pack_ref[PACK_ROWS + z : PACK_ROWS + z + 1, :] = edges(around)
    local_chain(list(range(STEPS)), b_ref, rhs_ref, None, None, r_ref, pack_ref, loc_ref)
    copy_pack(pack_refs)


def beside(ends, swapped):
    low = low_lanes(8)
    left = pltpu.roll(jnp.where(low, swapped, ends), 1, 0)
    right = pltpu.roll(jnp.where(low, ends, swapped), 7, 0)
    return left, right


def complete_edges(first, gather, coef_ref, halo_ref, inject_ref):
    low = low_lanes(8)
    known = [gather[:, t, :] for t in range(STEPS)]
    totals = [(row, swap_halves(row)) for row in known]
    for t in range(STEPS):
        halo = None if first and t == 0 else beside(*totals[t])
        if halo is None:
            halo_ref[t] = jnp.zeros((8, LANES), jnp.float32)
        else:
            halo_ref[t] = sum_x(jnp.where(low, *halo))
        if first:
            row = gather[:, PACK_ROWS + t, :]
            start = beside(row, swap_halves(row))
            halo = start if halo is None else [x + y for x, y in zip(halo, start)]
        reach = STEPS - 1 - t
        width = max(reach - 1, 1 if t == 0 else 0)
        if reach < 1:
            break
        summed = []
        for cells in halo:
            moved = {m: from_line(cells, m) for m in range(-width - 1, width + 2)}
            summed.append(
                {m: moved[m - 1] + moved[m] + moved[m + 1] for m in range(-width, width + 1)}
            )
        for n, (k, side, delta) in enumerate(SPREAD):
            if k <= reach:
                coef = coef_ref[:, STEPS + n, :]
                ends, swapped = totals[t + k]
                totals[t + k] = (
                    ends + coef * summed[side][delta],
                    swapped + swap_halves(coef) * summed[side][delta],
                )
        if t < 2:
            for n, (k, side, delta) in enumerate(SPREAD[: PLANES if t == 0 else 2]):
                inject_ref[t * PLANES + n] = summed[side][delta]


def ghost_pack_kernel(axis, own, ghost, *refs):
    *window_refs, ready_ref, out_ref = refs
    at = jnp.where(window_of(lax.axis_index(axis)) == 0, ghost, own)
    for k, ref in enumerate(window_refs):
        out_ref[k] = ref[:, :, pl.ds(pl.multiple_of(at, 8), ghost), :]


def next_kernel(steps, later, first, peers, axis, ghost, *refs):
    refs = list(refs)

    def take(count):
        taken = refs[:count]
        del refs[:count]
        return taken

    packs = take(peers)
    b_ref, plane_ref, rhs_in, loc_in = take(4)
    coef_ref, add_in, state_in = (None, None, None) if first else take(3)
    last = steps is not None and steps[-1] == 2 * rhs_in.shape[0] - 1
    if last:
        (out_ref,) = take(1)
        rhs_ref, state_ref, add_ref = rhs_in, None, refs.pop()
        add_ref[...] = add_in[...]
    else:
        rhs_ref, add_ref, state_ref = take(3)
    loc_ref, *pack_refs = take(peers) if later else (None,)
    coef_out = take(1)[0] if first else None
    gather, halo_ref, inject_ref, r_ref, *own_copy = refs
    nz = rhs_in.shape[0]
    position = lax.axis_index(axis)
    arrival = None
    if last:
        b_hbm, (b_ref, sems) = b_ref, own_copy
        size = 8 * LANES
        copies = [
            pltpu.make_async_copy(
                b_hbm.at[pl.ds(n * size, size)], b_ref.at[pl.ds(n * size, size)], sems.at[n]
            )
            for n in range(HALF // 8)
        ]
        for copy in copies:
            copy.start()

        def arrival(n):
            at = pl.ds(n * size, size)
            pltpu.make_async_copy(b_hbm.at[at], b_ref.at[at], sems.at[n]).wait()

    gather[...] = jnp.zeros(gather.shape, jnp.float32)
    for k in range(peers):
        gather[jnp.bitwise_xor(position, k)] = packs[k][: gather.shape[1], :]
    if first:
        coef_out[...] = gather[:, :PACK_ROWS, :]
    complete_edges(first, gather, gather if first else coef_ref, halo_ref, inject_ref)
    own = pl.ds(position, 1)
    low = low_lanes(HALF)
    row_index = lax.broadcasted_iota(jnp.int32, (HALF, LANES), 0)
    if first:
        for z in range(nz):
            row = gather[:, PACK_ROWS + z, :]
            left, right = beside(row, swap_halves(row))
            halo_ref[STEPS + z] = sum_x(jnp.where(low_lanes(8), left, right))
            halo = halo_ref[STEPS + z, own, :]
            at_edge = jnp.logical_or(
                jnp.logical_and(row_index == 0, low),
                jnp.logical_and(row_index == HALF - 1, jnp.logical_not(low)),
            )
            rhs_ref[z] = rhs_ref[z] + jnp.where(at_edge, halo, 0.0)

    first_plane, move = planes_of(steps, nz)

    def keep(z, state):
        add_ref[z] = 2.0 * state if move > 0 else state

    if not first:
        state = state_in[...]
        if move > 0:
            around = sum_y(sum_x(state), halo_ref[0, own, :])
            rhs_ref[first_plane - 1] = around - 27.0 * state
    state = loc_in[0]
    for n in range(2):
        state = state + plane_ref[n] * inject_ref[n, own, :]
    keep(first_plane, state)
    if move > 0:
        rhs_ref[first_plane] = sum_y(sum_x(state), halo_ref[1, own, :]) - 27.0 * state
    state = loc_in[1]
    for n in range(PLANES):
        state = state + plane_ref[n] * inject_ref[n if n >= 2 else PLANES + n, own, :]
    keep(first_plane + move, state)

    for t in range(2, STEPS):
        z = first_plane + move * t
        around = sum_y(sum_x(state), halo_ref[t, own, :])
        if move > 0:
            rhs_ref[z - 1] = around - 27.0 * state
        state = apply_blocks(b_ref, rhs_ref[z] + around, r_ref, arrival if t == 2 else None)
        if move < 0:
            state = state + add_ref[z]
        keep(z, state)
    if steps[-1] == nz - 1:
        rhs_ref[nz - 1] = -27.0 * state
    if not last:
        state_ref[...] = state
    if later:
        pack_ref = pack_refs[0]
        pack_ref[...] = jnp.zeros(pack_ref.shape, jnp.float32)
        local_chain(later, b_ref, rhs_ref, add_ref, state, r_ref, pack_ref, loc_ref)
        copy_pack(pack_refs)
    if last:
        own_lines = HALF - 2 * ghost
        for z in range(nz):
            plane = add_ref[z]
            turned = jnp.concatenate([plane, swap_halves(plane)], axis=0).T
            out_ref[z] = turned[ghost : ghost + own_lines]


def local_kernel(steps, b_ref, rhs_ref, add_ref, state_ref, loc_ref, *refs):
    *pack_refs, r_ref = refs
    pack_refs[0][...] = jnp.zeros(pack_refs[0].shape, jnp.float32)
    local_chain(steps, b_ref, rhs_ref, add_ref, state_ref[...], r_ref, pack_refs[0], loc_ref)
    copy_pack(pack_refs)


def finish_kernel(axis, v_ref, *refs):
    parts, out_ref = refs[:-1], refs[-1]
    position = lax.axis_index(axis)
    lines = parts[0].shape[1]
    for k, part in enumerate(parts):
        at = pl.ds(pl.multiple_of(window_of(jnp.bitwise_xor(position, k)) * lines, lines), lines)
        out_ref[:, at, :] = v_ref[:, at, :] + part[...]


def f32(*shape):
    return jax.ShapeDtypeStruct(shape, jnp.float32)


SMALL = pltpu.CompilerParams(vmem_limit_bytes=16 * 1024 * 1024)


def call(kernel, ins, outs, scratch, name, aliases=None, hbm=()):
    return pl.pallas_call(
        kernel,
        out_shape=outs,
        in_specs=[HBM if n in hbm else VMEM for n in range(len(ins))],
        out_specs=[VMEM] * len(outs),
        scratch_shapes=scratch,
        input_output_aliases=aliases or {},
        compiler_params=SMALL,
        name=name,
    )(*[in_hbm(x) if n in hbm else x for n, x in enumerate(ins)])


def in_hbm(a):
    return pltpu.with_memory_space_constraint(a, pltpu.HBM)


def to_peers(pieces, axis):
    count = lax.axis_size(axis)
    got = {0: pieces[0]}
    for k in reversed(range(1, count)):
        got[k] = lax.ppermute(pieces[k], axis, [(i, i ^ k) for i in range(count)])
    return [got[k] for k in range(count)]


def line_ghosts(cells, dim, width):
    count = lax.axis_size("gx")
    size = cells.shape[dim]
    head = lax.slice_in_dim(cells, 0, width, axis=dim)
    tail = lax.slice_in_dim(cells, size - width, size, axis=dim)
    if count == 2:
        at_first = lax.axis_index("gx") == 0
        other = lax.ppermute(jnp.where(at_first, tail, head), "gx", [(0, 1), (1, 0)])
        zero = jnp.zeros_like(other)
        return jnp.where(at_first, zero, other), jnp.where(at_first, other, zero)
    ups = [(i, i + 1) for i in range(count - 1)]
    downs = [(i + 1, i) for i in range(count - 1)]
    return lax.ppermute(tail, "gx", ups), lax.ppermute(head, "gx", downs)


def block_tail(blocks, width):
    groups, size = lax.axis_size("gz"), blocks.shape[0]
    start = jnp.where(lax.axis_index("gz") < groups // 2, size - width, 0)
    return lax.dynamic_slice_in_dim(blocks, start, width, 0)


def block_ghosts(tail, own):
    groups, count = lax.axis_size("gz"), lax.axis_size("gx")
    reach = -(-tail.shape[0] // own)
    assert 2 * reach <= groups
    pairs = []
    for strip in range(reach):
        low, high = window_of(strip), window_of(groups - 1 - strip)
        for a in range(count - 1):
            pairs.append((low * count + a, low * count + a + 1))
            pairs.append((high * count + a + 1, high * count + a))
    return lax.ppermute(tail, ("gz", "gx"), pairs)


def window_ghosts(windows, ready, own, ghost):
    groups, count = lax.axis_size("gz"), lax.axis_size("gx")
    nz_local = windows[0].shape[1]
    (lines,) = call(
        functools.partial(ghost_pack_kernel, "gz", own, ghost),
        [*windows, ready],
        [f32(groups, 2, nz_local, ghost, LANES)],
        [],
        "ghost_pack",
    )
    low, high = window_of(0) * count, window_of(groups - 1) * count
    pairs = [(high + a, low + a + 1) for a in range(count - 1)]
    pairs += [(low + a + 1, high + a) for a in range(count - 1)]
    return lax.ppermute(lines, ("gz", "gx"), pairs)


def refresh_ghosts(planes, ghost):
    split = planes.reshape(planes.shape[0], HALF, 2, HALF)
    groups, count = lax.axis_size("gz"), lax.axis_size("gx")
    places = [window_of(w) * count + x for x in range(count) for w in range(groups)]
    ups = list(zip(places[:-1], places[1:]))
    downs = list(zip(places[1:], places[:-1]))
    before = lax.ppermute(split[..., HALF - 2 * ghost : HALF - ghost], ("gz", "gx"), ups)
    after = lax.ppermute(split[..., ghost : 2 * ghost], ("gz", "gx"), downs)
    whole = jnp.concatenate([before, split[..., ghost : HALF - ghost], after], axis=-1)
    return whole.reshape(planes.shape)


def body(initial_field, source_term, block_inverse):
    groups, peers = lax.axis_size("gz"), lax.axis_size("gy")
    nz_local, lines, _ = initial_field.shape
    nz = nz_local * groups
    own = lines // groups
    ghost = (HALF - own) // 2
    assert block_inverse.shape[1:] == (LANES, LANES) and lines % groups == 0
    assert nz % STEPS == 0 and nz <= ghost and peers <= 4
    here = lax.axis_index("gz")

    late = own == 2 * ghost
    rows = block_inverse.reshape(lines * LANES, LANES)
    if late:
        chunks = HALF // ghost
        tail = pl.pallas_call(
            functools.partial(tail_kernel, "gz", groups),
            out_shape=f32(ghost, LANES, LANES),
            in_specs=[HBM],
            out_specs=VMEM,
            scratch_shapes=[pltpu.SemaphoreType.DMA((4,))],
            compiler_params=PARAMS,
            name="tail",
        )(in_hbm(block_inverse))
        windows = pl.pallas_call(
            functools.partial(pack_kernel, "gz", own, ghost),
            out_shape=[f32(2, nz_local, HALF, LANES)] * groups,
            in_specs=[HBM] * 2,
            out_specs=[VMEM] * groups,
            scratch_shapes=[pltpu.SemaphoreType.DMA((2 * groups * chunks,))],
            compiler_params=PARAMS,
            name="pack",
        )(in_hbm(initial_field), in_hbm(source_term))
    else:
        tail = block_tail(block_inverse, ghost)
        fields = jnp.stack([initial_field, source_term])
        before, after = line_ghosts(fields, 2, ghost)
        wide = jnp.concatenate([before, fields, after], axis=2)
        windows = [
            lax.dynamic_slice_in_dim(wide, window_of(jnp.bitwise_xor(here, k)) * own, HALF, 2)
            for k in range(groups)
        ]
    beyond = block_ghosts(tail, own).reshape(ghost * LANES, LANES)
    turned = LANES * HALF * LANES * 4
    if late:
        turn, sources = strip_kernel, [block_inverse]
        window, sems = (HALF, LANES, LANES), (4, 2, HALF // ghost)
    else:
        turn, sources = layout_kernel, [rows, beyond]
        window, sems = (HALF * LANES, LANES), (HALF // math.gcd(own, ghost),)
    blocks = pl.pallas_call(
        functools.partial(turn, own, ghost, "gz"),
        out_shape=f32(LANES * HALF, LANES),
        in_specs=[HBM] * len(sources),
        out_specs=VMEM,
        scratch_shapes=[pltpu.VMEM(window, jnp.float32), pltpu.SemaphoreType.DMA(sems)],
        compiler_params=PARAMS,
        cost_estimate=pl.CostEstimate(flops=0, bytes_accessed=4 * turned, transcendentals=0),
        name="layout",
    )(*[in_hbm(a) for a in sources])
    fields_here = to_peers(windows, "gz")
    ghosts_here = []
    plane = pltpu.VMEM((HALF, LANES), jnp.float32)

    def respond(at_end, ins, aliases=None):
        return call(
            functools.partial(responses_kernel, groups, at_end),
            ins,
            [f32(PACK_ROWS, LANES), f32(PLANES, HALF, LANES)],
            [plane, pltpu.VMEM((PLANES, HALF, LANES), jnp.float32)],
            "responses",
            aliases,
        )

    if late:
        early = respond(False, [blocks])
        ghosts_here = [window_ghosts(fields_here, early[0], own, ghost)]
        blocks = pl.pallas_call(
            functools.partial(patch_kernel, "gz", groups),
            out_shape=f32(LANES * HALF, LANES),
            in_specs=[VMEM] * 3,
            out_specs=VMEM,
            input_output_aliases={0: 0},
            compiler_params=PARAMS,
            name="patch",
        )(blocks, beyond, early[0])

    if late:
        answers, effects = respond(True, [blocks, *early], {1: 0, 2: 1})
    else:
        answers, effects = respond(None, [blocks])
    first_rows = PACK_ROWS + 8 * (-(-nz // 8))
    rhs, loc, *packs = call(
        functools.partial(first_kernel, "gz", groups, late),
        [*fields_here, *ghosts_here, blocks, answers],
        [f32(nz, HALF, LANES), f32(2, HALF, LANES)]
        + [f32(first_rows + 8 * k, LANES) for k in range(peers - 1)],
        [pltpu.VMEM((nz + 2, HALF, LANES), jnp.float32), pltpu.VMEM((nz, HALF, LANES), jnp.float32)]
        + [plane],
        "first_chain",
    )
    schedule = [list(range(a, a + STEPS)) for a in range(0, 2 * nz, STEPS)]
    coef = add = state = None
    for n, steps in enumerate(schedule):
        first = n == 0
        final = n + 1 == len(schedule)
        renew = steps[-1] == nz - 1 and 2 * nz > ghost
        later = None if final or renew else schedule[n + 1]
        packs = to_peers([packs[0], *packs], "gy")
        ins = [*packs, blocks, effects, rhs, loc] + ([] if first else [coef, add, state])
        planes = f32(nz, HALF, LANES)
        outs = [f32(nz, own, LANES)] if final else [planes, planes, f32(HALF, LANES)]
        if later:
            outs += [f32(2, HALF, LANES)] + [f32(8 * k, LANES) for k in range(1, peers)]
        outs += [f32(8, PACK_ROWS, LANES)] if first else []
        aliases = {} if final else {peers + 2: 0}
        if not first and not final:
            aliases[peers + 5] = 1
        results = call(
            functools.partial(next_kernel, steps, later, first, peers, "gy", ghost),
            ins,
            outs,
            [
                pltpu.VMEM((8, first_rows if first else 8, LANES), jnp.float32),
                pltpu.VMEM((STEPS + nz, 8, LANES), jnp.float32),
                pltpu.VMEM((PLANES + 2, 8, LANES), jnp.float32),
                plane,
            ]
            + (
                [
                    pltpu.VMEM((LANES * HALF, LANES), jnp.float32),
                    pltpu.SemaphoreType.DMA((HALF // 8,)),
                    pltpu.VMEM((nz, HALF, LANES), jnp.float32),
                ]
                if final
                else []
            ),
            "next_chain",
            aliases,
            (peers,) if final else (),
        )
        if final:
            change = results[0]
            break
        rhs, add, state = results[:3]
        if later:
            loc, *packs = results[3 : 3 + peers]
        if first:
            coef = results[-1]
        if renew:
            renewed = refresh_ghosts(jnp.concatenate([rhs, add, state[None]]), ghost)
            rhs, add, state = renewed[:nz], renewed[nz : 2 * nz], renewed[2 * nz]
            loc, *packs = call(
                functools.partial(local_kernel, schedule[n + 1]),
                [blocks, rhs, add, state],
                [f32(2, HALF, LANES)] + [f32(8 * k, LANES) for k in range(1, peers)],
                [plane],
                "local_chain",
            )

    sends = [
        lax.dynamic_slice_in_dim(change, jnp.bitwise_xor(here, k) * nz_local, nz_local, 0)
        for k in range(groups)
    ]
    parts = to_peers(sends, "gz")
    return call(
        functools.partial(finish_kernel, "gz"),
        [initial_field, *parts],
        [f32(*initial_field.shape)],
        [],
        "finish",
    )[0]


def solution(mesh):
    placed = (P("gz", "gx", "gy"), P("gz", "gx", "gy"), P("gx", "gy", None))
    return jax.shard_map(
        body, mesh=mesh, in_specs=placed, out_specs=P("gz", "gx", "gy"), check_vma=False
    )
```

```python
import functools
import math
import jax
import jax.numpy as jnp
from jax import lax
from jax.experimental import pallas as pl
from jax.experimental.pallas import tpu as pltpu
from jax.sharding import PartitionSpec as P

LANES = 128
HALF = 64
STEPS = 4
SPREAD = [(k, side, delta) for k in range(1, STEPS) for side in range(2) for delta in range(1 - k, k)]
PLANES = sum(k <= 2 for k, _, _ in SPREAD)
PACK_ROWS = 8 * (-(-(STEPS + len(SPREAD)) // 8))
VMEM = pl.BlockSpec(memory_space=pltpu.VMEM)
HBM = pl.BlockSpec(memory_space=pltpu.HBM)
PARAMS = pltpu.CompilerParams(vmem_limit_bytes=16 * 1024 * 1024)


def window_of(device):
    if isinstance(device, int):
        return device ^ 1 if device < 2 else device
    return jnp.where(device < 2, jnp.bitwise_xor(device, 1), device)


def low_lanes(rows):
    return lax.broadcasted_iota(jnp.int32, (rows, LANES), 1) < HALF


def swap_halves(a):
    return pltpu.roll(a, HALF, 1)


def from_line(a, delta):
    return a if delta == 0 else pltpu.roll(a, (-delta) % LANES, 1)


def sum_x(a):
    return a + pltpu.roll(a, 1, 1) + pltpu.roll(a, LANES - 1, 1)


def sum_y(a, halo=None):
    low = low_lanes(1)
    first = swap_halves(a[:8])[0:1]
    last = swap_halves(a[HALF - 8 :])[7:8]
    halo = jnp.zeros((1, LANES), jnp.float32) if halo is None else halo
    above = jnp.where(low, halo, last)
    below = jnp.where(low, first, halo)
    row = lax.broadcasted_iota(jnp.int32, a.shape, 0)
    up = jnp.where(row == 0, above, pltpu.roll(a, 1, 0))
    down = jnp.where(row == HALF - 1, below, pltpu.roll(a, HALF - 1, 0))
    return a + up + down


def spread(a):
    low = low_lanes(a.shape[0])
    swapped = swap_halves(a)
    return jnp.where(low, a, swapped), jnp.where(low, swapped, a)


def edges(a):
    return jnp.where(low_lanes(1), a[0:1], a[HALF - 1 : HALF])


def block_column(b_ref, j):
    return b_ref[pl.ds(j, HALF, stride=LANES), :]


def fold_rows(parts):
    row = lax.broadcasted_iota(jnp.int32, (8, LANES), 0)
    for bit in (1, 2, 4):
        first = (row & bit) == 0
        parts = [
            jnp.where(first, a, b) + pltpu.roll(jnp.where(first, b, a), 8 - bit, 0)
            for a, b in zip(parts[::2], parts[1::2])
        ]
    return parts[0]


def apply_blocks(b_ref, rhs, out_ref, arrival=None):
    tiles = [half[8 * t : 8 * t + 8] for half in spread(rhs) for t in range(HALF // 8)]

    def rows(outer, carry):
        if arrival is not None:
            arrival(outer)
        parts = []
        for u in range(8):
            at = (outer * 8 + u) * LANES
            terms = [b_ref[pl.ds(at + 8 * t, 8), :] * tiles[t] for t in range(2)]
            for t in range(2, len(tiles)):
                terms[t % 2] = terms[t % 2] + b_ref[pl.ds(at + 8 * t, 8), :] * tiles[t]
            parts.append(terms[0] + terms[1])
        out_ref[pl.ds(outer * 8, 8), :] = fold_rows(parts)
        return carry

    lax.fori_loop(0, HALF // 8, rows, 0, unroll=True)
    return out_ref[...]


def edge_rows(b_ref):
    return jnp.where(
        low_lanes(LANES), b_ref[0:LANES, :], b_ref[(HALF - 1) * LANES : HALF * LANES, :]
    )


def apply_edges(rows, rhs):
    top, bottom = spread(rhs)
    return jnp.sum(rows[:HALF] * top + rows[HALF:] * bottom, axis=0, keepdims=True)


def layout_kernel(own, ghost, axis, b_ref, *refs):
    *ghost_refs, out_ref, window, sems = refs
    ghost_ref = ghost_refs[0] if ghost_refs else b_ref
    count = b_ref.shape[0] // LANES
    position = window_of(lax.axis_index(axis))
    chunk = math.gcd(own, ghost)
    size = chunk * LANES
    copies = []
    for c in range(HALF // chunk):
        start = position * own - ghost + c * chunk
        inside = jnp.logical_and(start >= 0, start < count)
        target = window.at[pl.ds(c * size, size)]
        here = jnp.clip(start, 0, count - chunk)
        beyond = jnp.clip(jnp.where(start < 0, start + ghost, start - count), 0, ghost - chunk)

        @pl.when(inside)
        def _(at=pl.multiple_of(here * LANES, LANES), target=target, c=c):
            pltpu.make_async_copy(b_ref.at[pl.ds(at, size)], target, sems.at[c]).start()

        @pl.when(jnp.logical_not(inside))
        def _(at=pl.multiple_of(beyond * LANES, LANES), target=target, c=c):
            pltpu.make_async_copy(ghost_ref.at[pl.ds(at, size)], target, sems.at[c]).start()

        copies.append(pltpu.make_async_copy(b_ref.at[pl.ds(0, size)], target, sems.at[c]))
    for copy in copies:
        copy.wait()

    lax.fori_loop(0, HALF // 8, functools.partial(turn_rows, window, out_ref), 0)


def turn_rows(window, out_ref, outer, carry):
    for u in range(8):
        i = outer * 8 + u
        top = window[pl.ds(i, HALF, stride=LANES), :]
        bottom = window[pl.ds(i + HALF, HALF, stride=LANES), :]
        at = pl.multiple_of(i * LANES, LANES)
        out_ref[pl.ds(at, LANES), :] = jnp.concatenate([top, bottom], axis=0).T
    return carry


def strip_kernel(own, ghost, axis, b_ref, out_ref, window, sems):
    position = window_of(lax.axis_index(axis))
    parts = sems.shape[0]
    size = HALF // parts
    copies = [[] for _ in range(parts)]
    for n in range(parts):
        for half in range(2):
            rows = pl.ds(half * HALF + n * size, size)
            for c in range(HALF // ghost):
                at = jnp.clip(position * own - ghost + c * ghost, 0, b_ref.shape[0] - ghost)
                copies[n].append(
                    pltpu.make_async_copy(
                        b_ref.at[pl.ds(at, ghost), rows, :],
                        window.at[pl.ds(c * ghost, ghost), rows, :],
                        sems.at[n, half, c],
                    )
                )
    for copy in sum(copies, []):
        copy.start()
    flat = window.reshape(HALF * LANES, LANES)
    for n in range(parts):
        for copy in copies[n]:
            copy.wait()
        turn = functools.partial(turn_rows, flat, out_ref)
        lax.fori_loop(n * size // 8, (n + 1) * size // 8, turn, 0)


def tail_kernel(axis, groups, b_ref, tail_ref, sems):
    ghost = tail_ref.shape[0]
    start = jnp.where(lax.axis_index(axis) < groups // 2, b_ref.shape[0] - ghost, 0)
    part = ghost // 4
    copies = [
        pltpu.make_async_copy(
            b_ref.at[pl.ds(start + n * part, part)], tail_ref.at[pl.ds(n * part, part)], sems.at[n]
        )
        for n in range(4)
    ]
    for copy in copies:
        copy.start()
    for copy in copies:
        copy.wait()


def pack_kernel(axis, own, ghost, v_ref, s_ref, *refs):
    *window_refs, sems = refs
    position = lax.axis_index(axis)
    last = v_ref.shape[1] - ghost
    copies = []
    for k, window_ref in enumerate(window_refs):
        peer = window_of(jnp.bitwise_xor(position, k))
        for c in range(HALF // ghost):
            at = pl.multiple_of(jnp.clip(peer * own - ghost + c * ghost, 0, last), ghost)
            for kind, ref in enumerate((v_ref, s_ref)):
                copies.append(
                    pltpu.make_async_copy(
                        ref.at[:, pl.ds(at, ghost), :],
                        window_ref.at[kind, :, pl.ds(c * ghost, ghost), :],
                        sems.at[len(copies)],
                    )
                )
    for copy in copies:
        copy.start()
    for copy in copies:
        copy.wait()


def patch_kernel(axis, groups, b_in, beyond, early_ref, out_ref):
    ghost = beyond.shape[0] // LANES
    per_turn = HALF // ghost
    unroll = 4
    position = window_of(lax.axis_index(axis))
    for place, at in ((0, 0), (groups - 1, HALF - ghost)):

        @pl.when(position == place)
        def _(at=at):
            lane = lax.broadcasted_iota(jnp.int32, (LANES, LANES), 1) % HALF
            mine = jnp.logical_and(lane >= at, lane < at + ghost)

            def one(outer, carry):
                turns = []
                for v in range(unroll):
                    first = (outer * unroll + v) * per_turn
                    rows = [
                        beyond[pl.ds(half * HALF + first + u, ghost, stride=LANES), :]
                        for half in range(2)
                        for u in range(per_turn)
                    ]
                    turns.append(jnp.concatenate(rows, axis=0).T)
                for v in range(unroll):
                    first = (outer * unroll + v) * per_turn
                    for u in range(per_turn):
                        moved = from_line(turns[v], (u * ghost - at) % LANES)
                        here = pl.ds(pl.multiple_of((first + u) * LANES, LANES), LANES)
                        out_ref[here, :] = jnp.where(mine, moved, b_in[here, :])
                return carry

            lax.fori_loop(0, HALF // per_turn // unroll, one, 0)


def responses_kernel(groups, at_end, b_ref, *refs):
    pack_ref, plane_ref, r_ref, many_ref = refs[-4:]
    if at_end is None:
        responses(b_ref, pack_ref, plane_ref, r_ref, many_ref)
        return
    window = window_of(lax.axis_index("gz"))
    ends = jnp.logical_or(window == 0, window == groups - 1)

    @pl.when(ends if at_end else jnp.logical_not(ends))
    def _():
        responses(b_ref, pack_ref, plane_ref, r_ref, many_ref)


def responses(b_ref, pack_ref, plane_ref, r_ref, many_ref):
    pack_ref[...] = jnp.zeros(pack_ref.shape, jnp.float32)
    firsts = [block_column(b_ref, 0), block_column(b_ref, LANES - 1)]
    for side, first in enumerate(firsts):
        many_ref[side] = first
        shifted = sum_y(first)
        for n, (k, at_side, delta) in enumerate(SPREAD):
            if k == 2 and at_side == side:
                many_ref[n] = from_line(shifted, delta)

    def product(n, carry):
        many_ref[n] = apply_blocks(b_ref, many_ref[n], r_ref)
        return carry

    lax.fori_loop(2, PLANES, product, 0, unroll=True)
    second = {SPREAD[n][1:]: many_ref[n] for n in range(2, PLANES)}
    rows = edge_rows(b_ref)
    for n, (k, side, delta) in enumerate(SPREAD):
        if k <= 2:
            row = edges(many_ref[n])
        else:
            parts = [
                from_line(second[side, delta - m], m) for m in (-1, 0, 1) if abs(delta - m) <= 1
            ]
            row = apply_edges(rows, sum_y(sum(parts[1:], parts[0])))
        pack_ref[pl.ds(STEPS + n, 1), :] = row
    plane_ref[...] = many_ref[...]


def planes_of(steps, nz):
    return (steps[0], 1) if steps[0] < nz else (2 * nz - 1 - steps[0], -1)


def local_chain(steps, b_ref, rhs_ref, add_ref, state, r_ref, pack_ref, loc_ref):
    first, move = planes_of(steps, rhs_ref.shape[0])
    if state is None:
        state = jnp.zeros((HALF, LANES), jnp.float32)
    else:
        pack_ref[0:1, :] = edges(state)
    ahead = len(steps) - 2

    def transition(n, state):
        z = first + move * n
        state = apply_blocks(b_ref, rhs_ref[z] + sum_y(sum_x(state)), r_ref)
        if move < 0:
            state = state + add_ref[z]
        loc_ref[n] = state
        pack_ref[pl.ds(n + 1, 1), :] = edges(state)
        return state

    state = lax.fori_loop(0, ahead, transition, state, unroll=True)
    z = first + move * ahead
    row = apply_edges(edge_rows(b_ref), rhs_ref[z] + sum_y(sum_x(state)))
    pack_ref[ahead + 1 : ahead + 2, :] = row + edges(add_ref[z]) if move < 0 else row


def copy_pack(pack_refs):
    first = pack_refs[0][...]
    for ref in pack_refs[1:]:
        ref[: first.shape[0], :] = first
        ref[first.shape[0] :, :] = jnp.zeros((ref.shape[0] - first.shape[0], LANES), jnp.float32)


def gather_planes(axis, groups, field_refs, ghost_ref, v_ref, s_ref):
    position = lax.axis_index(axis)
    window = window_of(position)
    senders = window_of(0) ^ window_of(groups - 1)
    low = low_lanes(HALF)
    nz_local = field_refs[0].shape[1]
    for k, ref in enumerate(field_refs):
        base = jnp.bitwise_xor(position, k) * nz_local
        for p in range(nz_local):
            for kind, target in ((0, v_ref), (1, s_ref)):
                plane = ref[kind, p]
                if ghost_ref is not None:
                    beyond = ghost_ref[senders ^ k, kind, p]
                    ghost = beyond.shape[0]
                    first = jnp.where(window == 0, beyond, plane[:ghost])
                    last = jnp.where(window == groups - 1, beyond, plane[HALF - ghost :])
                    plane = jnp.concatenate([first, plane[ghost : HALF - ghost], last], axis=0)
                turned = jnp.concatenate([plane, plane], axis=0).T
                target[base + p + 1 - kind] = jnp.where(low, turned[:HALF], turned[HALF:])


def first_kernel(axis, fields, late, *refs):
    field_refs = refs[:fields]
    ghost_ref = refs[fields] if late else None
    refs = refs[1:] if late else refs
    b_ref, answers_ref, rhs_ref, loc_ref, *pack_refs, v_ref, s_ref, r_ref = refs[fields:]
    pack_ref = pack_refs[0]
    nz = rhs_ref.shape[0]
    pack_ref[...] = jnp.zeros(pack_ref.shape, jnp.float32)
    pack_ref[:PACK_ROWS, :] = answers_ref[...]
    v_ref[0] = jnp.zeros((HALF, LANES), jnp.float32)
    v_ref[nz + 1] = jnp.zeros((HALF, LANES), jnp.float32)
    gather_planes(axis, fields, field_refs, ghost_ref, v_ref, s_ref)
    for z in range(nz):
        around = v_ref[z] + v_ref[z + 1] + v_ref[z + 2]
        rhs_ref[z] = s_ref[z] - 27.0 * v_ref[z + 1] + sum_y(sum_x(around))
        pack_ref[PACK_ROWS + z : PACK_ROWS + z + 1, :] = edges(around)
    local_chain(list(range(STEPS)), b_ref, rhs_ref, None, None, r_ref, pack_ref, loc_ref)
    copy_pack(pack_refs)


def beside(ends, swapped):
    low = low_lanes(8)
    left = pltpu.roll(jnp.where(low, swapped, ends), 1, 0)
    right = pltpu.roll(jnp.where(low, ends, swapped), 7, 0)
    return left, right


def complete_edges(first, gather, coef_ref, halo_ref, inject_ref):
    low = low_lanes(8)
    known = [gather[:, t, :] for t in range(STEPS)]
    totals = [(row, swap_halves(row)) for row in known]
    for t in range(STEPS):
        halo = None if first and t == 0 else beside(*totals[t])
        if halo is None:
            halo_ref[t] = jnp.zeros((8, LANES), jnp.float32)
        else:
            halo_ref[t] = sum_x(jnp.where(low, *halo))
        if first:
            row = gather[:, PACK_ROWS + t, :]
            start = beside(row, swap_halves(row))
            halo = start if halo is None else [x + y for x, y in zip(halo, start)]
        reach = STEPS - 1 - t
        width = max(reach - 1, 1 if t == 0 else 0)
        if reach < 1:
            break
        summed = []
        for cells in halo:
            moved = {m: from_line(cells, m) for m in range(-width - 1, width + 2)}
            summed.append(
                {m: moved[m - 1] + moved[m] + moved[m + 1] for m in range(-width, width + 1)}
            )
        for n, (k, side, delta) in enumerate(SPREAD):
            if k <= reach:
                coef = coef_ref[:, STEPS + n, :]
                ends, swapped = totals[t + k]
                totals[t + k] = (
                    ends + coef * summed[side][delta],
                    swapped + swap_halves(coef) * summed[side][delta],
                )
        if t < 2:
            for n, (k, side, delta) in enumerate(SPREAD[: PLANES if t == 0 else 2]):
                inject_ref[t * PLANES + n] = summed[side][delta]


def ghost_pack_kernel(axis, own, ghost, *refs):
    *window_refs, ready_ref, out_ref = refs
    at = jnp.where(window_of(lax.axis_index(axis)) == 0, ghost, own)
    for k, ref in enumerate(window_refs):
        out_ref[k] = ref[:, :, pl.ds(pl.multiple_of(at, 8), ghost), :]


def next_kernel(steps, later, first, peers, axis, ghost, *refs):
    refs = list(refs)

    def take(count):
        taken = refs[:count]
        del refs[:count]
        return taken

    packs = take(peers)
    b_ref, plane_ref, rhs_in, loc_in = take(4)
    coef_ref, add_in, state_in = (None, None, None) if first else take(3)
    last = steps is not None and steps[-1] == 2 * rhs_in.shape[0] - 1
    if last:
        (out_ref,) = take(1)
        rhs_ref, state_ref, add_ref = rhs_in, None, refs.pop()
        add_ref[...] = add_in[...]
    else:
        rhs_ref, add_ref, state_ref = take(3)
    loc_ref, *pack_refs = take(peers) if later else (None,)
    coef_out = take(1)[0] if first else None
    gather, halo_ref, inject_ref, r_ref, *own_copy = refs
    nz = rhs_in.shape[0]
    position = lax.axis_index(axis)
    arrival = None
    if last:
        b_hbm, (b_ref, sems) = b_ref, own_copy
        size = 8 * LANES
        copies = [
            pltpu.make_async_copy(
                b_hbm.at[pl.ds(n * size, size)], b_ref.at[pl.ds(n * size, size)], sems.at[n]
            )
            for n in range(HALF // 8)
        ]
        for copy in copies:
            copy.start()

        def arrival(n):
            at = pl.ds(n * size, size)
            pltpu.make_async_copy(b_hbm.at[at], b_ref.at[at], sems.at[n]).wait()

    gather[...] = jnp.zeros(gather.shape, jnp.float32)
    for k in range(peers):
        gather[jnp.bitwise_xor(position, k)] = packs[k][: gather.shape[1], :]
    if first:
        coef_out[...] = gather[:, :PACK_ROWS, :]
    complete_edges(first, gather, gather if first else coef_ref, halo_ref, inject_ref)
    own = pl.ds(position, 1)
    low = low_lanes(HALF)
    row_index = lax.broadcasted_iota(jnp.int32, (HALF, LANES), 0)
    if first:
        for z in range(nz):
            row = gather[:, PACK_ROWS + z, :]
            left, right = beside(row, swap_halves(row))
            halo_ref[STEPS + z] = sum_x(jnp.where(low_lanes(8), left, right))
            halo = halo_ref[STEPS + z, own, :]
            at_edge = jnp.logical_or(
                jnp.logical_and(row_index == 0, low),
                jnp.logical_and(row_index == HALF - 1, jnp.logical_not(low)),
            )
            rhs_ref[z] = rhs_ref[z] + jnp.where(at_edge, halo, 0.0)

    first_plane, move = planes_of(steps, nz)

    def keep(z, state):
        add_ref[z] = 2.0 * state if move > 0 else state

    if not first:
        state = state_in[...]
        if move > 0:
            around = sum_y(sum_x(state), halo_ref[0, own, :])
            rhs_ref[first_plane - 1] = around - 27.0 * state
    state = loc_in[0]
    for n in range(2):
        state = state + plane_ref[n] * inject_ref[n, own, :]
    keep(first_plane, state)
    if move > 0:
        rhs_ref[first_plane] = sum_y(sum_x(state), halo_ref[1, own, :]) - 27.0 * state
    state = loc_in[1]
    for n in range(PLANES):
        state = state + plane_ref[n] * inject_ref[n if n >= 2 else PLANES + n, own, :]
    keep(first_plane + move, state)

    for t in range(2, STEPS):
        z = first_plane + move * t
        around = sum_y(sum_x(state), halo_ref[t, own, :])
        if move > 0:
            rhs_ref[z - 1] = around - 27.0 * state
        state = apply_blocks(b_ref, rhs_ref[z] + around, r_ref, arrival if t == 2 else None)
        if move < 0:
            state = state + add_ref[z]
        keep(z, state)
    if steps[-1] == nz - 1:
        rhs_ref[nz - 1] = -27.0 * state
    if not last:
        state_ref[...] = state
    if later:
        pack_ref = pack_refs[0]
        pack_ref[...] = jnp.zeros(pack_ref.shape, jnp.float32)
        local_chain(later, b_ref, rhs_ref, add_ref, state, r_ref, pack_ref, loc_ref)
        copy_pack(pack_refs)
    if last:
        own_lines = HALF - 2 * ghost
        for z in range(nz):
            plane = add_ref[z]
            turned = jnp.concatenate([plane, swap_halves(plane)], axis=0).T
            out_ref[z] = turned[ghost : ghost + own_lines]


def local_kernel(steps, b_ref, rhs_ref, add_ref, state_ref, loc_ref, *refs):
    *pack_refs, r_ref = refs
    pack_refs[0][...] = jnp.zeros(pack_refs[0].shape, jnp.float32)
    local_chain(steps, b_ref, rhs_ref, add_ref, state_ref[...], r_ref, pack_refs[0], loc_ref)
    copy_pack(pack_refs)


def finish_kernel(axis, v_ref, *refs):
    parts, out_ref = refs[:-1], refs[-1]
    position = lax.axis_index(axis)
    lines = parts[0].shape[1]
    for k, part in enumerate(parts):
        at = pl.ds(pl.multiple_of(window_of(jnp.bitwise_xor(position, k)) * lines, lines), lines)
        out_ref[:, at, :] = v_ref[:, at, :] + part[...]


def f32(*shape):
    return jax.ShapeDtypeStruct(shape, jnp.float32)


SMALL = pltpu.CompilerParams(vmem_limit_bytes=16 * 1024 * 1024)


def call(kernel, ins, outs, scratch, name, aliases=None, hbm=()):
    return pl.pallas_call(
        kernel,
        out_shape=outs,
        in_specs=[HBM if n in hbm else VMEM for n in range(len(ins))],
        out_specs=[VMEM] * len(outs),
        scratch_shapes=scratch,
        input_output_aliases=aliases or {},
        compiler_params=SMALL,
        name=name,
    )(*[in_hbm(x) if n in hbm else x for n, x in enumerate(ins)])


def in_hbm(a):
    return pltpu.with_memory_space_constraint(a, pltpu.HBM)


def to_peers(pieces, axis):
    count = lax.axis_size(axis)
    got = {0: pieces[0]}
    for k in reversed(range(1, count)):
        got[k] = lax.ppermute(pieces[k], axis, [(i, i ^ k) for i in range(count)])
    return [got[k] for k in range(count)]


def line_ghosts(cells, dim, width):
    count = lax.axis_size("gx")
    size = cells.shape[dim]
    head = lax.slice_in_dim(cells, 0, width, axis=dim)
    tail = lax.slice_in_dim(cells, size - width, size, axis=dim)
    if count == 2:
        at_first = lax.axis_index("gx") == 0
        other = lax.ppermute(jnp.where(at_first, tail, head), "gx", [(0, 1), (1, 0)])
        zero = jnp.zeros_like(other)
        return jnp.where(at_first, zero, other), jnp.where(at_first, other, zero)
    ups = [(i, i + 1) for i in range(count - 1)]
    downs = [(i + 1, i) for i in range(count - 1)]
    return lax.ppermute(tail, "gx", ups), lax.ppermute(head, "gx", downs)


def block_tail(blocks, width):
    groups, size = lax.axis_size("gz"), blocks.shape[0]
    start = jnp.where(lax.axis_index("gz") < groups // 2, size - width, 0)
    return lax.dynamic_slice_in_dim(blocks, start, width, 0)


def block_ghosts(tail, own):
    groups, count = lax.axis_size("gz"), lax.axis_size("gx")
    reach = -(-tail.shape[0] // own)
    assert 2 * reach <= groups
    pairs = []
    for strip in range(reach):
        low, high = window_of(strip), window_of(groups - 1 - strip)
        for a in range(count - 1):
            pairs.append((low * count + a, low * count + a + 1))
            pairs.append((high * count + a + 1, high * count + a))
    return lax.ppermute(tail, ("gz", "gx"), pairs)


def window_ghosts(windows, ready, own, ghost):
    groups, count = lax.axis_size("gz"), lax.axis_size("gx")
    nz_local = windows[0].shape[1]
    (lines,) = call(
        functools.partial(ghost_pack_kernel, "gz", own, ghost),
        [*windows, ready],
        [f32(groups, 2, nz_local, ghost, LANES)],
        [],
        "ghost_pack",
    )
    low, high = window_of(0) * count, window_of(groups - 1) * count
    pairs = [(high + a, low + a + 1) for a in range(count - 1)]
    pairs += [(low + a + 1, high + a) for a in range(count - 1)]
    return lax.ppermute(lines, ("gz", "gx"), pairs)


def refresh_ghosts(planes, ghost):
    split = planes.reshape(planes.shape[0], HALF, 2, HALF)
    groups, count = lax.axis_size("gz"), lax.axis_size("gx")
    places = [window_of(w) * count + x for x in range(count) for w in range(groups)]
    ups = list(zip(places[:-1], places[1:]))
    downs = list(zip(places[1:], places[:-1]))
    before = lax.ppermute(split[..., HALF - 2 * ghost : HALF - ghost], ("gz", "gx"), ups)
    after = lax.ppermute(split[..., ghost : 2 * ghost], ("gz", "gx"), downs)
    whole = jnp.concatenate([before, split[..., ghost : HALF - ghost], after], axis=-1)
    return whole.reshape(planes.shape)


def body(initial_field, source_term, block_inverse):
    groups, peers = lax.axis_size("gz"), lax.axis_size("gy")
    nz_local, lines, _ = initial_field.shape
    nz = nz_local * groups
    own = lines // groups
    ghost = (HALF - own) // 2
    assert block_inverse.shape[1:] == (LANES, LANES) and lines % groups == 0
    assert nz % STEPS == 0 and nz <= ghost and peers <= 4
    here = lax.axis_index("gz")

    late = own == 2 * ghost
    rows = block_inverse.reshape(lines * LANES, LANES)
    if late:
        chunks = HALF // ghost
        tail = pl.pallas_call(
            functools.partial(tail_kernel, "gz", groups),
            out_shape=f32(ghost, LANES, LANES),
            in_specs=[HBM],
            out_specs=VMEM,
            scratch_shapes=[pltpu.SemaphoreType.DMA((4,))],
            compiler_params=PARAMS,
            name="tail",
        )(in_hbm(block_inverse))
        windows = pl.pallas_call(
            functools.partial(pack_kernel, "gz", own, ghost),
            out_shape=[f32(2, nz_local, HALF, LANES)] * groups,
            in_specs=[HBM] * 2,
            out_specs=[VMEM] * groups,
            scratch_shapes=[pltpu.SemaphoreType.DMA((2 * groups * chunks,))],
            compiler_params=PARAMS,
            name="pack",
        )(in_hbm(initial_field), in_hbm(source_term))
    else:
        tail = block_tail(block_inverse, ghost)
        fields = jnp.stack([initial_field, source_term])
        before, after = line_ghosts(fields, 2, ghost)
        wide = jnp.concatenate([before, fields, after], axis=2)
        windows = [
            lax.dynamic_slice_in_dim(wide, window_of(jnp.bitwise_xor(here, k)) * own, HALF, 2)
            for k in range(groups)
        ]
    beyond = block_ghosts(tail, own).reshape(ghost * LANES, LANES)
    turned = LANES * HALF * LANES * 4
    if late:
        turn, sources = strip_kernel, [block_inverse]
        window, sems = (HALF, LANES, LANES), (8, 2, HALF // ghost)
    else:
        turn, sources = layout_kernel, [rows, beyond]
        window, sems = (HALF * LANES, LANES), (HALF // math.gcd(own, ghost),)
    blocks = pl.pallas_call(
        functools.partial(turn, own, ghost, "gz"),
        out_shape=f32(LANES * HALF, LANES),
        in_specs=[HBM] * len(sources),
        out_specs=VMEM,
        scratch_shapes=[pltpu.VMEM(window, jnp.float32), pltpu.SemaphoreType.DMA(sems)],
        compiler_params=PARAMS,
        cost_estimate=pl.CostEstimate(flops=0, bytes_accessed=4 * turned, transcendentals=0),
        name="layout",
    )(*[in_hbm(a) for a in sources])
    fields_here = to_peers(windows, "gz")
    ghosts_here = []
    plane = pltpu.VMEM((HALF, LANES), jnp.float32)

    def respond(at_end, ins, aliases=None):
        return call(
            functools.partial(responses_kernel, groups, at_end),
            ins,
            [f32(PACK_ROWS, LANES), f32(PLANES, HALF, LANES)],
            [plane, pltpu.VMEM((PLANES, HALF, LANES), jnp.float32)],
            "responses",
            aliases,
        )

    if late:
        early = respond(False, [blocks])
        ghosts_here = [window_ghosts(fields_here, early[0], own, ghost)]
        blocks = pl.pallas_call(
            functools.partial(patch_kernel, "gz", groups),
            out_shape=f32(LANES * HALF, LANES),
            in_specs=[VMEM] * 3,
            out_specs=VMEM,
            input_output_aliases={0: 0},
            compiler_params=PARAMS,
            name="patch",
        )(blocks, beyond, early[0])

    if late:
        answers, effects = respond(True, [blocks, *early], {1: 0, 2: 1})
    else:
        answers, effects = respond(None, [blocks])
    first_rows = PACK_ROWS + 8 * (-(-nz // 8))
    rhs, loc, *packs = call(
        functools.partial(first_kernel, "gz", groups, late),
        [*fields_here, *ghosts_here, blocks, answers],
        [f32(nz, HALF, LANES), f32(2, HALF, LANES)]
        + [f32(first_rows + 8 * k, LANES) for k in range(peers - 1)],
        [pltpu.VMEM((nz + 2, HALF, LANES), jnp.float32), pltpu.VMEM((nz, HALF, LANES), jnp.float32)]
        + [plane],
        "first_chain",
    )
    schedule = [list(range(a, a + STEPS)) for a in range(0, 2 * nz, STEPS)]
    coef = add = state = None
    for n, steps in enumerate(schedule):
        first = n == 0
        final = n + 1 == len(schedule)
        renew = steps[-1] == nz - 1 and 2 * nz > ghost
        later = None if final or renew else schedule[n + 1]
        packs = to_peers([packs[0], *packs], "gy")
        ins = [*packs, blocks, effects, rhs, loc] + ([] if first else [coef, add, state])
        planes = f32(nz, HALF, LANES)
        outs = [f32(nz, own, LANES)] if final else [planes, planes, f32(HALF, LANES)]
        if later:
            outs += [f32(2, HALF, LANES)] + [f32(8 * k, LANES) for k in range(1, peers)]
        outs += [f32(8, PACK_ROWS, LANES)] if first else []
        aliases = {} if final else {peers + 2: 0}
        if not first and not final:
            aliases[peers + 5] = 1
        results = call(
            functools.partial(next_kernel, steps, later, first, peers, "gy", ghost),
            ins,
            outs,
            [
                pltpu.VMEM((8, first_rows if first else 8, LANES), jnp.float32),
                pltpu.VMEM((STEPS + nz, 8, LANES), jnp.float32),
                pltpu.VMEM((PLANES + 2, 8, LANES), jnp.float32),
                plane,
            ]
            + (
                [
                    pltpu.VMEM((LANES * HALF, LANES), jnp.float32),
                    pltpu.SemaphoreType.DMA((HALF // 8,)),
                    pltpu.VMEM((nz, HALF, LANES), jnp.float32),
                ]
                if final
                else []
            ),
            "next_chain",
            aliases,
            (peers,) if final else (),
        )
        if final:
            change = results[0]
            break
        rhs, add, state = results[:3]
        if later:
            loc, *packs = results[3 : 3 + peers]
        if first:
            coef = results[-1]
        if renew:
            renewed = refresh_ghosts(jnp.concatenate([rhs, add, state[None]]), ghost)
            rhs, add, state = renewed[:nz], renewed[nz : 2 * nz], renewed[2 * nz]
            loc, *packs = call(
                functools.partial(local_kernel, schedule[n + 1]),
                [blocks, rhs, add, state],
                [f32(2, HALF, LANES)] + [f32(8 * k, LANES) for k in range(1, peers)],
                [plane],
                "local_chain",
            )

    sends = [
        lax.dynamic_slice_in_dim(change, jnp.bitwise_xor(here, k) * nz_local, nz_local, 0)
        for k in range(groups)
    ]
    parts = to_peers(sends, "gz")
    return call(
        functools.partial(finish_kernel, "gz"),
        [initial_field, *parts],
        [f32(*initial_field.shape)],
        [],
        "finish",
    )[0]


def solution(mesh):
    placed = (P("gz", "gx", "gy"), P("gz", "gx", "gy"), P("gx", "gy", None))
    return jax.shard_map(
        body, mesh=mesh, in_specs=placed, out_specs=P("gz", "gx", "gy"), check_vma=False
    )
```
